32 devices in a mesh: gy: 4 (over z), gx: 8 (over y, x, core).
Axes of the slice: x: 2, y: 2, z: 4, core: 2. Of those that a mesh axis runs over, the one named last changes fastest.
Arguments:
- saved_thickness: bfloat16 [2, 256, 2048], P(None, 'gy', 'gx'), may hold values from 0.5 to 2
- saved_velocity: bfloat16 [2, 2, 256, 2048], P(None, None, 'gy', 'gx'), may hold values from -4 to 4
- surface_slope: bfloat16 [2, 256, 2048], P(None, 'gy', 'gx'), may hold values from -3 to 3
- basal_beta: float32 [256, 2048], P('gy', 'gx'), may hold values from 0.2 to 5
- cell_mask: int32 [256, 2048], P('gy', 'gx'), may hold values from 0 to 2
- upwind_flags: int32 [256, 2048], P('gy', 'gx'), may hold values from 0 to 3
- observed_velocity: bfloat16 [2, 2, 256, 2048], P(None, None, 'gy', 'gx'), may hold values from -60 to 60
- thickness_adjoint: float32 [256, 2048], P('gy', 'gx'), may hold values from -6 to 6
Outputs:
- beta_gradient: float32 [256, 2048], P('gy', 'gx')
- thickness_gradient: float32 [256, 2048], P('gy', 'gx')
- misfit: float32 [], replicated
The draws below stay inside these ranges and needn't reach their ends.
All inputs are finite; a program needn't handle non-finite values.
Results may differ from the reference program's by a relative error of at most 0.0003.
Values sent between devices are 32-bit elements; how exact they have to be, the bound alone decides.
A program may use at most 64 MiB of HBM per device.

```python
import math
import jax
import jax.numpy as jnp
from jax import lax

SWEEPS = 3
STEPS = 2
NY = 256
NX = 2048


def draw_observed_velocity(key, part):
    row_ramp = 1.0 + 2.0 * jnp.arange(NY, dtype=jnp.float32) / NY
    col_ramp = 1.0 + 2.0 * jnp.arange(NX, dtype=jnp.float32) / NX
    ramp_field = row_ramp[:, None] * col_ramp[None, :]
    noise = jnp.clip(jax.random.normal(key, (STEPS, 2, NY, NX), jnp.float32), -4.0, 4.0)
    return (noise * ramp_field[None, None]).astype(jnp.bfloat16)


def place_ends(drawn, own_key, smallest, high):
    place = [jax.random.randint(jax.random.fold_in(own_key, axis), (), 0, length) for axis, length in enumerate(drawn.shape)]
    main_axis = drawn.shape.index(max(drawn.shape))
    beside = place[:main_axis] + [(place[main_axis] + 1) % drawn.shape[main_axis]] + place[main_axis + 1:]
    return drawn.at[tuple(place)].set(smallest).at[tuple(beside)].set(high)


def block_scale(own_key, extent, cuts, least, high):
    def one(axis_at, blocks):
        heights = jax.random.uniform(jax.random.fold_in(jax.random.fold_in(own_key, 6), axis_at), (blocks,), jnp.float32, least / len(cuts), high / len(cuts))
        return jnp.repeat(jnp.exp(heights), extent[axis_at] // blocks).reshape((-1,) + (1,) * (len(extent) - axis_at - 1))

    factor_of = one(*cuts[0])
    for cut in cuts[1:]:
        factor_of = factor_of * one(*cut)
    return factor_of


def gaussian(rng, extent, width, most, split=(), kind=jnp.bfloat16):
    array = width * jax.random.normal(rng, extent, jnp.float32)
    if split:
        array = array * block_scale(rng, extent, split, -0.22, 0.18)
    return jnp.clip(array, -most, most).astype(kind)


def setup_inputs(seed: int = 0) -> dict:
    splits = jax.random.split(jax.random.key(seed), 9)
    return {
        "saved_thickness": jnp.clip(0.5 + 1.5 * jax.random.uniform(splits[0], (STEPS, NY, NX), jnp.float32) ** block_scale(splits[0], (STEPS, NY, NX), ((1, 4), (2, 8)), -0.2, 0.2), 0.5, 2.0).astype(jnp.bfloat16),
        "saved_velocity": gaussian(splits[1], (STEPS, 2, NY, NX), 1.0, 4.0, ((2, 4), (3, 8))),
        "surface_slope": gaussian(splits[2], (2, NY, NX), 0.5, 3.0, ((1, 4), (2, 8))),
        "basal_beta": jnp.clip(jnp.exp(math.log(5.0) - 3.218876 * jax.random.uniform(splits[3], (NY, NX), jnp.float32) ** block_scale(splits[3], (NY, NX), ((0, 4), (1, 8)), -0.2, 0.2)), 0.2, 5.0),
        "cell_mask": place_ends(jax.random.randint(splits[4], (NY, NX), 0, 3), jax.random.fold_in(splits[4], 1), 0, 2).astype(jnp.int32),
        "upwind_flags": place_ends(jax.random.randint(splits[5], (NY, NX), 0, 4), jax.random.fold_in(splits[5], 1), 0, 3).astype(jnp.int32),
        "observed_velocity": draw_observed_velocity(jax.random.fold_in(splits[8], 71), 0),
        "thickness_adjoint": gaussian(splits[7], (NY, NX), 1.0, 6.0, ((0, 4), (1, 8)), jnp.float32),
    }


RELAXATION = 0.8
TIME_STEP = 0.1
EPSILON = 1e-06
OFFSETS = ((0, 1), (2, 1), (1, 0), (1, 2))

def shifted(padded, row_offset, col_offset):
    row_count = padded.shape[-2] - 2
    col_count = padded.shape[-1] - 2
    return padded[..., row_offset:row_offset + row_count, col_offset:col_offset + col_count]

def sweep_core(velocity_pad, thick_pad, cover_pad, friction, forcing):
    center = shifted(velocity_pad, 1, 1)
    thick_mid = shifted(thick_pad, 1, 1)
    cover_mid = shifted(cover_pad, 1, 1)
    flux_sum = jnp.zeros_like(center)
    coupling_sum = jnp.zeros_like(thick_mid)
    for row_offset, col_offset in OFFSETS:
        difference = shifted(velocity_pad, row_offset, col_offset) - center
        strain = lax.optimization_barrier(jnp.sum(difference * difference, axis=0))
        coupling = 0.5 * (thick_mid + shifted(thick_pad, row_offset, col_offset)) * cover_mid * shifted(cover_pad, row_offset, col_offset) * jnp.power(1.0 + strain, -1.0 / 3.0)
        flux_sum = flux_sum + coupling * difference
        coupling_sum = coupling_sum + coupling
    residual = forcing - friction * center + flux_sum
    return cover_mid * (center + RELAXATION * residual / (1.0 + friction + coupling_sum))

def transport_core(thick_pad, velocity_pad, cover_pad, donor_east_pad, donor_south_pad):
    east_cover = cover_pad[1:-1, :-1] * cover_pad[1:-1, 1:]
    speed_east = 0.5 * (velocity_pad[0, 1:-1, :-1] + velocity_pad[0, 1:-1, 1:])
    donor_east = donor_east_pad[1:-1, :-1]
    flux_east = speed_east * east_cover * (donor_east * thick_pad[1:-1, :-1] + (1.0 - donor_east) * thick_pad[1:-1, 1:])
    south_cover = cover_pad[:-1, 1:-1] * cover_pad[1:, 1:-1]
    speed_south = 0.5 * (velocity_pad[1, :-1, 1:-1] + velocity_pad[1, 1:, 1:-1])
    donor_south = donor_south_pad[:-1, 1:-1]
    flux_south = speed_south * south_cover * (donor_south * thick_pad[:-1, 1:-1] + (1.0 - donor_south) * thick_pad[1:, 1:-1])
    diverge = flux_east[:, 1:] - flux_east[:, :-1] + flux_south[1:, :] - flux_south[:-1, :]
    return cover_pad[1:-1, 1:-1] * (thick_pad[1:-1, 1:-1] - TIME_STEP * diverge)

def pad_one(values):
    widths = [(0, 0)] * (values.ndim - 2) + [(1, 1), (1, 1)]
    return jnp.pad(values, widths)

def forward_step(thickness, friction, initial_guess, slope_field, cover_pad, donor_east_pad, donor_south_pad):
    forcing = thickness * slope_field
    thick_pad = pad_one(thickness)
    velocity = initial_guess
    sweep_step = jax.checkpoint(sweep_core)
    for sweep_index in range(SWEEPS):
        velocity = sweep_step(pad_one(velocity), thick_pad, cover_pad, friction, forcing)
    thick_next = jax.checkpoint(transport_core)(thick_pad, pad_one(velocity), cover_pad, donor_east_pad, donor_south_pad)
    return (velocity, thick_next)

def reference(saved_thickness, saved_velocity, surface_slope, basal_beta, cell_mask, upwind_flags, observed_velocity, thickness_adjoint):
    cover = (cell_mask > 0).astype(jnp.float32)
    grounded = (cell_mask == 2).astype(jnp.float32)
    friction = basal_beta * grounded
    slope_field = surface_slope.astype(jnp.float32)
    cover_pad = pad_one(cover)
    donor_east_pad = pad_one((upwind_flags % 2).astype(jnp.float32))
    donor_south_pad = pad_one((upwind_flags // 2).astype(jnp.float32))
    cotangent = thickness_adjoint
    beta_gradient = jnp.zeros_like(basal_beta)
    misfit = jnp.zeros((), jnp.float32)
    for step_index in reversed(range(STEPS)):
        initial_guess = saved_velocity[step_index].astype(jnp.float32)
        observed = observed_velocity[step_index].astype(jnp.float32)
        misfit_scale = jnp.mean(grounded * lax.optimization_barrier(jnp.sum(observed * observed, axis=0))) + EPSILON

        def advance(thickness, friction_field):
            return forward_step(thickness, friction_field, initial_guess, slope_field, cover_pad, donor_east_pad, donor_south_pad)
        (velocity, thick_next), pullback = jax.vjp(advance, saved_thickness[step_index].astype(jnp.float32), friction)
        difference = velocity - observed
        misfit_field = grounded * difference
        misfit = misfit + 0.5 * jnp.mean(lax.optimization_barrier(jnp.sum(misfit_field * difference, axis=0))) / misfit_scale
        cotangent, friction_bar = pullback((misfit_field / misfit_scale, cotangent))
        beta_gradient = beta_gradient + grounded * friction_bar
    return (beta_gradient, cotangent, misfit)
```

```python
import jax
import jax.numpy as jnp
from jax import lax
from jax.experimental import pallas as pl
from jax.experimental.pallas import tpu as pltpu
from jax.sharding import PartitionSpec as P

RELAXATION = 0.8
TIME_STEP = 0.1
EPSILON = 1e-06
MESH = pl.DeviceIdType.MESH

RIM = 2
COLS = 16

MASK, BETA, SLU, SLV, H1, U1, V1 = range(7)
DEEP = 7
FLAGS, H0, U0, V0, OU0, OV0, OU1, OV1, ADJ = range(7, 16)
FIELDS = 16

STATIC = ("cov", "gr", "fri", "cce", "ccs", "de", "ds")
STEP = ("ce", "cs", "u1", "v1", "u2", "v2", "u3", "v3")
SWEEP = ("pe", "ps", "deu", "dev", "dsu", "dsv", "yu", "yv", "inv")
BACK = ("qu", "qv", "e", "bu", "bv")
REST = ("hce", "hcs", "hacc", "facc", "g1", "f1", "g0", "f0")


def scratch_names():
    names = list(STATIC)
    for n in range(2):
        names += [f"{n}{name}" for name in STEP]
        for j in range(3):
            names += [f"{n}{j}{name}" for name in SWEEP]
    for b in range(2):
        names += [f"b{b}{name}" for name in BACK]
    return names + list(REST)


NAMES = scratch_names()


def make_kernel(ny, nx, rows, cols, cell_count):
    strips = rows // 8
    total = strips + 2 * RIM
    first, last = RIM - 1, RIM + strips + 1
    width = cols + 128

    def kernel(
        thick_hbm, vel_hbm, slope_hbm, beta_hbm, mask_hbm, flags_hbm, obs_hbm, adj_hbm,
        beta_out, thick_out, misfit_out,
        fld, col_send, col_recv, sum_x, sum_y, send_sem, recv_sem,
        sx_send, sx_recv, sy_send, sy_recv, in_sem,
        thick_in, vel_in, slope_in, beta_in, mask_in, flags_in, obs_in, adj_in, *refs,
    ):
        pairs = (
            (mask_hbm, mask_in), (beta_hbm, beta_in), (slope_hbm, slope_in), (thick_hbm, thick_in),
            (vel_hbm, vel_in), (flags_hbm, flags_in), (obs_hbm, obs_in), (adj_hbm, adj_in),
        )
        loads = [
            pltpu.make_async_copy(src, dst, in_sem.at[i]) for i, (src, dst) in enumerate(pairs)
        ]
        for load in loads:
            load.start()
        s = dict(zip(NAMES, refs))
        gy, gx = lax.axis_index("gy"), lax.axis_index("gx")
        centre = slice(RIM, RIM + strips)

        def exists(dy, dx):
            ok = None
            for move, at, count in ((dy, gy, ny), (dx, gx, nx)):
                if move:
                    here = at > 0 if move < 0 else at < count - 1
                    ok = here if ok is None else jnp.logical_and(ok, here)
            return ok

        diagonals = ((-1, -1), (-1, 1), (1, -1), (1, 1))
        sides = ((-1, 0), (1, 0), (0, -1), (0, 1))

        zero_rows = jnp.zeros((FIELDS, 2, 8, cols), jnp.float32)
        fld[:, 0:RIM, :, 0:cols] = zero_rows
        fld[:, RIM + strips : total, :, 0:cols] = zero_rows
        col_recv[...] = jnp.zeros_like(col_recv)

        barrier = pltpu.get_barrier_semaphore()
        for off in range(1, nx):
            pl.semaphore_signal(
                barrier, inc=1, device_id=(gy, lax.rem(gx + off, nx)), device_id_type=MESH
            )
        for off in range(1, ny):
            pl.semaphore_signal(
                barrier, inc=1, device_id=(lax.rem(gy + off, ny), gx), device_id_type=MESH
            )
        for dy, dx in diagonals:

            @pl.when(exists(dy, dx))
            def _():
                pl.semaphore_signal(
                    barrier, inc=1, device_id=(gy + dy, gx + dx), device_id_type=MESH
                )

        def place(field, value):
            fld[field, centre, :, 0:cols] = value.astype(jnp.float32).reshape(strips, 8, cols)

        for load in loads:
            load.wait()
        place(MASK, mask_in[...])
        place(BETA, beta_in[...])
        place(SLU, slope_in[0])
        place(SLV, slope_in[1])
        place(H1, thick_in[1])
        place(U1, vel_in[1, 0])
        place(V1, vel_in[1, 1])
        place(FLAGS, flags_in[...])
        place(H0, thick_in[0])
        place(U0, vel_in[0, 0])
        place(V0, vel_in[0, 1])
        place(OU0, obs_in[0, 0])
        place(OV0, obs_in[0, 1])
        place(OU1, obs_in[1, 0])
        place(OV1, obs_in[1, 1])
        place(ADJ, adj_in[...])

        lane = lax.broadcasted_iota(jnp.int32, (8, 128), 1)
        sub = lax.broadcasted_iota(jnp.int32, (8, width), 0)

        for n, (ou, ov) in enumerate(((OU0, OV0), (OU1, OV1))):
            def scale_body(k, acc, ou=ou, ov=ov):
                a, b = fld[ou, k, :, 0:cols], fld[ov, k, :, 0:cols]
                t = jnp.where(fld[MASK, k, :, 0:cols] == 2.0, a * a + b * b, 0.0)
                for c in range(0, cols, 128):
                    acc = acc + t[:, c : c + 128]
                return acc

            sum_x[0, 0, n] = lax.fori_loop(
                RIM, RIM + strips, scale_body, jnp.zeros((8, 128), jnp.float32)
            )

        def pack_body(k, _):
            for side, at in ((0, 0), (1, cols - 128)):
                for tile in range(FIELDS * COLS // 128):
                    packed = jnp.zeros((8, 128), jnp.float32)
                    for i in range(128 // COLS):
                        x = fld[tile * (128 // COLS) + i, k + RIM, :, at : at + 128]
                        move = (i * COLS - (0 if side == 0 else 128 - COLS)) % 128
                        if move:
                            x = pltpu.roll(x, move, 1)
                        inside = jnp.logical_and(lane >= i * COLS, lane < (i + 1) * COLS)
                        packed = jnp.where(inside, x, packed)
                    col_send[side, k, :, tile * 128 : (tile + 1) * 128] = packed
            return 0

        lax.fori_loop(0, strips, pack_body, 0)

        beside = [
            jnp.where(at > 0, 1, 0) + jnp.where(at < count - 1, 1, 0)
            for at, count in ((gy, ny), (gx, nx))
        ]
        pl.semaphore_wait(barrier, (nx - 1) + (ny - 1) + beside[0] * beside[1])

        hi = RIM + strips
        plan = []
        for i, (dy, dx) in enumerate(sides):
            if dy:
                src = slice(RIM, RIM + 2) if dy < 0 else slice(hi - 2, hi)
                dst = slice(hi, hi + 2) if dy < 0 else slice(0, 2)
                plan.append(
                    (dy, dx, fld.at[0:DEEP, src, :, 0:cols], fld.at[0:DEEP, dst, :, 0:cols])
                )
                src = slice(RIM, RIM + 1) if dy < 0 else slice(hi - 1, hi)
                dst = slice(hi, hi + 1) if dy < 0 else slice(1, 2)
                plan.append(
                    (dy, dx, fld.at[DEEP:FIELDS, src, :, 0:cols], fld.at[DEEP:FIELDS, dst, :, 0:cols])
                )
            else:
                side = 0 if dx < 0 else 1
                plan.append((dy, dx, col_send.at[side], col_recv.at[side, centre]))
        for dy, dx in diagonals:
            side = 0 if dx < 0 else 1
            src = slice(0, 2) if dy < 0 else slice(strips - 2, strips)
            dst = slice(hi, hi + 2) if dy < 0 else slice(0, 2)
            plan.append((dy, dx, col_send.at[side, src], col_recv.at[side, dst]))
        copies = []
        for i, (dy, dx, src, dst) in enumerate(plan):
            copy = pltpu.make_async_remote_copy(
                src_ref=src, dst_ref=dst, send_sem=send_sem.at[i], recv_sem=recv_sem.at[i],
                device_id=(gy + dy, gx + dx), device_id_type=MESH,
            )
            copies.append((dy, dx, copy))

            @pl.when(exists(dy, dx))
            def _():
                copy.start()

        def spread(which, axis):
            buf, ssem, rsem, count = (
                (sum_x, sx_send, sx_recv, nx) if axis == "gx" else (sum_y, sy_send, sy_recv, ny)
            )
            made = []
            for off in range(1, count):
                peer = (
                    (gy, lax.rem(gx + off, nx)) if axis == "gx" else (lax.rem(gy + off, ny), gx)
                )
                made.append(
                    pltpu.make_async_remote_copy(
                        src_ref=buf.at[which, 0], dst_ref=buf.at[which, off],
                        send_sem=ssem.at[which, off], recv_sem=rsem.at[which, off],
                        device_id=peer, device_id_type=MESH,
                    )
                )
            return made

        def added(which, axis, n):
            buf, me, count = (sum_x, gx, nx) if axis == "gx" else (sum_y, gy, ny)
            acc = jnp.zeros((8, 128), jnp.float32)
            for src in range(count):
                acc = acc + buf[which, lax.rem(me - src + count, count), n]
            return acc

        def whole(tile):
            return jnp.sum(jnp.sum(tile, axis=1, keepdims=True), axis=0, keepdims=True)

        scale_x = spread(0, "gx")
        for copy in scale_x:
            copy.start()

        for copy in scale_x:
            copy.wait()
        for n in range(2):
            sum_y[0, 0, n] = added(0, "gx", n)
        scale_y = spread(0, "gy")
        for copy in scale_y:
            copy.start()

        for dy, dx, copy in copies:

            @pl.when(exists(-dy, -dx))
            def _():
                copy.wait_recv()

        def unpack_body(k, _):
            for tile in range(FIELDS * COLS // 128):
                nxt = col_recv[0, k, :, tile * 128 : (tile + 1) * 128]
                prv = col_recv[1, k, :, tile * 128 : (tile + 1) * 128]
                for i in range(128 // COLS):
                    a = pltpu.roll(nxt, (-i * COLS) % 128, 1) if i else nxt
                    move = (128 - COLS - i * COLS) % 128
                    b = pltpu.roll(prv, move, 1) if move else prv
                    both = jnp.where(lane < COLS, a, jnp.where(lane >= 128 - COLS, b, 0.0))
                    fld[tile * (128 // COLS) + i, k, :, cols:width] = both
            return 0

        lax.fori_loop(0, total, unpack_body, 0)

        def east(x):
            return pltpu.roll(x, width - 1, 1)

        def west(x):
            return pltpu.roll(x, 1, 1)

        def south(cur, nxt):
            return pltpu.roll(jnp.where(sub == 0, nxt, cur), 7, 0)

        def north(prev, cur):
            return pltpu.roll(jnp.where(sub == 7, prev, cur), 1, 0)

        zero = jnp.zeros((8, width), jnp.float32)

        def after(k):
            return jnp.minimum(k + 1, total - 1)

        def static_body(k, _):
            mask = fld[MASK, k]
            cov = jnp.where(mask > 0.0, 1.0, 0.0)
            cov_n = jnp.where(fld[MASK, after(k)] > 0.0, 1.0, 0.0)
            gr = jnp.where(mask == 2.0, 1.0, 0.0)
            cce = 0.5 * cov * east(cov)
            ccs = 0.5 * cov * south(cov, cov_n)
            flags = fld[FLAGS, k]
            ds = jnp.where(flags >= 2.0, 1.0, 0.0)
            s["cov"][k] = cov
            s["gr"][k] = gr
            s["fri"][k] = fld[BETA, k] * gr
            s["cce"][k] = cce
            s["ccs"][k] = ccs
            s["ds"][k] = ds
            s["de"][k] = flags - 2.0 * ds
            for n, h in ((0, H0), (1, H1)):
                hh = fld[h, k]
                s[f"{n}ce"][k] = cce * (hh + east(hh))
                s[f"{n}cs"][k] = ccs * (hh + south(hh, fld[h, after(k)]))
            return 0

        lax.fori_loop(0, total, static_body, 0)

        H = (H0, H1)
        W = ((U0, V0), (U1, V1))

        def velocity(n, j):
            if j == 0:
                return fld.at[W[n][0]], fld.at[W[n][1]]
            return s[f"{n}u{j}"], s[f"{n}v{j}"]

        def edge_zero(names):
            for name in names:
                for k in (first - 1, last):
                    s[name][k] = zero

        edge_zero([f"{n}{c}{j}" for n in range(2) for j in (1, 2, 3) for c in "uv"])
        edge_zero([f"b{b}{c}" for b in range(2) for c in ("qu", "qv", "e")] + ["g1"])

        def forward(n, j, lo, end):
            u_ref, v_ref = velocity(n, j)
            u_to, v_to = velocity(n, j + 1)
            t = {name: s[f"{n}{j}{name}"] for name in SWEEP}

            def body(k, carry):
                pfu, pfv, pc = carry
                kn = after(k)
                u, v = u_ref[k], v_ref[k]
                deu, dev = east(u) - u, east(v) - v
                dsu, dsv = south(u, u_ref[kn]) - u, south(v, v_ref[kn]) - v
                pe = jnp.exp(jnp.log(1.0 + (deu * deu + dev * dev)) * (-1.0 / 3.0))
                ps = jnp.exp(jnp.log(1.0 + (dsu * dsu + dsv * dsv)) * (-1.0 / 3.0))
                ce, cs = s[f"{n}ce"][k] * pe, s[f"{n}cs"][k] * ps
                feu, fev, fsu, fsv = ce * deu, ce * dev, cs * dsu, cs * dsv
                fri, h = s["fri"][k], fld[H[n], k]
                inv = 1.0 / (1.0 + fri + ((ce + west(ce)) + (cs + north(pc, cs))))
                ru = h * fld[SLU, k] - fri * u + ((feu - west(feu)) + (fsu - north(pfu, fsu)))
                rv = h * fld[SLV, k] - fri * v + ((fev - west(fev)) + (fsv - north(pfv, fsv)))
                yu, yv = ru * inv, rv * inv
                cov = s["cov"][k]
                u_to[k] = cov * (u + RELAXATION * yu)
                v_to[k] = cov * (v + RELAXATION * yv)
                for name, value in zip(SWEEP, (pe, ps, deu, dev, dsu, dsv, yu, yv, inv)):
                    t[name][k] = value
                return fsu, fsv, cs

            lax.fori_loop(lo, end, body, (zero, zero, zero))

        forward(1, 0, 0, total)
        forward(1, 1, first, last)
        forward(1, 2, first, last)
        forward(0, 0, first, last)
        forward(0, 1, first, last)
        forward(0, 2, first, last)

        O = ((OU0, OV0), (OU1, OV1))
        for n in range(2):
            def misfit_body(k, acc, n=n):
                a = s[f"{n}u3"][k, :, 0:cols] - fld[O[n][0], k, :, 0:cols]
                b = s[f"{n}v3"][k, :, 0:cols] - fld[O[n][1], k, :, 0:cols]
                t = s["gr"][k, :, 0:cols] * (a * a + b * b)
                for c in range(0, cols, 128):
                    acc = acc + t[:, c : c + 128]
                return acc

            sum_x[1, 0, n] = 0.5 * lax.fori_loop(
                RIM, RIM + strips, misfit_body, jnp.zeros((8, 128), jnp.float32)
            )
        misfit_x = spread(1, "gx")
        for copy in misfit_x:
            copy.start()

        for copy in scale_y:
            copy.wait()
        scales = [whole(added(0, "gy", n)) * (1.0 / cell_count) + EPSILON for n in range(2)]

        def emit(n, j, b, k, lu, lv):
            cov, fri = s["cov"][k], s["fri"][k]
            au, av = cov * lu, cov * lv
            inv = RELAXATION * s[f"{n}{j}inv"][k]
            qu, qv = au * inv, av * inv
            s[f"b{b}qu"][k] = qu
            s[f"b{b}qv"][k] = qv
            s[f"b{b}e"][k] = -(qu * s[f"{n}{j}yu"][k] + qv * s[f"{n}{j}yv"][k])
            s[f"b{b}bu"][k] = au - fri * qu
            s[f"b{b}bv"][k] = av - fri * qv

        def transport(n, g_ref):
            per_scale = jnp.broadcast_to(1.0 / scales[n], (8, width))

            def body(k, carry):
                pvs, phs = carry
                kn = k + 1
                g, gn = s["cov"][k] * g_ref[k], s["cov"][kn] * g_ref[kn]
                h, hn = fld[H[n], k], fld[H[n], kn]
                u, v = s[f"{n}u3"][k], s[f"{n}v3"][k]
                de, ds = s["de"][k], s["ds"][k]
                pse = (TIME_STEP * s["cce"][k]) * (east(g) - g)
                pss = (TIME_STEP * s["ccs"][k]) * (south(g, gn) - g)
                ue = pse * (de * h + (1.0 - de) * east(h))
                vs = pss * (ds * h + (1.0 - ds) * south(h, hn))
                he = pse * (u + east(u))
                hs = pss * (v + south(v, s[f"{n}v3"][kn]))
                he_here, hs_here = de * he, ds * hs
                he_there, hs_there = he - he_here, hs - hs_here
                seed = s["gr"][k] * per_scale
                lu = seed * (u - fld[O[n][0], k]) + (ue + west(ue))
                lv = seed * (v - fld[O[n][1], k]) + (vs + north(pvs, vs))
                s["hacc"][k] = g + (he_here + west(he_there)) + (hs_here + north(phs, hs_there))
                emit(n, 2, 0, k, lu, lv)
                return vs, hs_there

            lax.fori_loop(first, last, body, (zero, zero))

        def backward(n, j, b, end, g_to=None, f_to=None):
            u_ref, v_ref = velocity(n, j)
            t = {name: s[f"{n}{j}{name}"] for name in SWEEP}
            q = {name: s[f"b{b}{name}"] for name in BACK}
            start, finish = j == 2, j == 0

            def body(k, carry):
                kn = k + 1
                qu, qv, e = q["qu"][k], q["qv"][k], q["e"][k]
                feu, fev = qu - east(qu), qv - east(qv)
                fsu, fsv = qu - south(qu, q["qu"][kn]), qv - south(qv, q["qv"][kn])
                pe, ps = t["pe"][k], t["ps"][k]
                deu, dev, dsu, dsv = t["deu"][k], t["dev"][k], t["dsu"][k], t["dsv"][k]
                ke = (feu * deu + fev * dev) + (e + east(e))
                ks = (fsu * dsu + fsv * dsv) + (e + south(e, q["e"][kn]))
                kpe, kps = ke * pe, ks * ps
                f = e - (qu * u_ref[k] + qv * v_ref[k])
                h = qu * fld[SLU, k] + qv * fld[SLV, k] + s["hacc"][k]
                if not start:
                    kpe_sum, kps_sum = s["hce"][k] + kpe, s["hcs"][k] + kps
                    f = f + s["facc"][k]
                else:
                    kpe_sum, kps_sum = kpe, kps
                if finish:
                    ge, gs = s["cce"][k] * kpe_sum, s["ccs"][k] * kps_sum
                    g_to[k] = h + ((ge + west(ge)) + (gs + north(carry[0], gs)))
                    f_to[k] = f
                    return (gs,)
                s["hce"][k] = kpe_sum
                s["hcs"][k] = kps_sum
                s["facc"][k] = f
                s["hacc"][k] = h
                ce, cs = s[f"{n}ce"][k] * pe, s[f"{n}cs"][k] * ps
                te = (2.0 / 3.0) * ce * (pe * pe) * kpe
                ts = (2.0 / 3.0) * cs * (ps * ps) * kps
                xeu, xev = ce * feu - te * deu, ce * fev - te * dev
                xsu, xsv = cs * fsu - ts * dsu, cs * fsv - ts * dsv
                lu = q["bu"][k] + ((west(xeu) - xeu) + (north(carry[0], xsu) - xsu))
                lv = q["bv"][k] + ((west(xev) - xev) + (north(carry[1], xsv) - xsv))
                emit(n, j - 1, 1 - b, k, lu, lv)
                return xsu, xsv

            lax.fori_loop(first, end, body, (zero,) if finish else (zero, zero))

        transport(1, fld.at[ADJ])
        backward(1, 2, 0, last)
        backward(1, 1, 1, last)
        backward(1, 0, 0, last, s["g1"], s["f1"])

        for copy in misfit_x:
            copy.wait()
        for n in range(2):
            sum_y[1, 0, n] = added(1, "gx", n)
        misfit_y = spread(1, "gy")
        for copy in misfit_y:
            copy.start()

        transport(0, s["g1"])
        backward(0, 2, 0, last)
        backward(0, 1, 1, last)
        backward(0, 0, 0, last - 1, s["g0"], s["f0"])

        f_sum = s["f1"][centre, :, 0:cols] + s["f0"][centre, :, 0:cols]
        beta_out[...] = s["gr"][centre, :, 0:cols] * f_sum
        thick_out[...] = s["g0"][centre, :, 0:cols]

        for copy in misfit_y:
            copy.wait()
        parts = [whole(added(1, "gy", n)) * (1.0 / cell_count) / scales[n] for n in range(2)]
        misfit_out[...] = parts[1] + parts[0]
        for dy, dx, copy in copies:

            @pl.when(exists(dy, dx))
            def _():
                copy.wait_send()

    return kernel


def on_device(*args):
    ny, nx = lax.axis_size("gy"), lax.axis_size("gx")
    rows, cols = args[3].shape
    strips = rows // 8
    total = strips + 2 * RIM
    width = cols + 128
    vmem = pl.BlockSpec(memory_space=pltpu.VMEM)
    dma = pltpu.SemaphoreType.DMA
    beta, thick, misfit = pl.pallas_call(
        make_kernel(ny, nx, rows, cols, rows * cols * ny * nx),
        out_shape=(
            jax.ShapeDtypeStruct((strips, 8, cols), jnp.float32),
            jax.ShapeDtypeStruct((strips, 8, cols), jnp.float32),
            jax.ShapeDtypeStruct((1, 1), jnp.float32),
        ),
        in_specs=[pl.BlockSpec(memory_space=pltpu.HBM)] * len(args),
        out_specs=(vmem, vmem, vmem),
        scratch_shapes=[
            pltpu.VMEM((FIELDS, total, 8, width), jnp.float32),
            pltpu.VMEM((2, strips, 8, FIELDS * COLS), jnp.float32),
            pltpu.VMEM((2, total, 8, FIELDS * COLS), jnp.float32),
            pltpu.VMEM((2, nx, 2, 8, 128), jnp.float32),
            pltpu.VMEM((2, ny, 2, 8, 128), jnp.float32),
            dma((10,)), dma((10,)),
            dma((2, nx)), dma((2, nx)), dma((2, ny)), dma((2, ny)), dma((len(args),)),
        ]
        + [pltpu.VMEM(arg.shape, arg.dtype) for arg in args]
        + [pltpu.VMEM((total, 8, width), jnp.float32)] * len(NAMES),
        compiler_params=pltpu.CompilerParams(
            collective_id=0, has_side_effects=True, vmem_limit_bytes=62 * 1024 * 1024
        ),
    )(*args)
    return beta.reshape(rows, cols), thick.reshape(rows, cols), misfit.reshape(())


def solution(mesh):
    in_specs = (
        P(None, "gy", "gx"),
        P(None, None, "gy", "gx"),
        P(None, "gy", "gx"),
        P("gy", "gx"),
        P("gy", "gx"),
        P("gy", "gx"),
        P(None, None, "gy", "gx"),
        P("gy", "gx"),
    )
    out_specs = (P("gy", "gx"), P("gy", "gx"), P())
    return jax.shard_map(
        on_device, mesh=mesh, in_specs=in_specs, out_specs=out_specs, check_vma=False
    )
```

```python
import jax
import jax.numpy as jnp
from jax import lax
from jax.experimental import pallas as pl
from jax.experimental.pallas import tpu as pltpu
from jax.sharding import PartitionSpec as P

RELAXATION = 0.8
TIME_STEP = 0.1
EPSILON = 1e-06
MESH = pl.DeviceIdType.MESH

RIM = 2
COLS = 16

MASK, BETA, SLU, SLV, H1, U1, V1 = range(7)
DEEP = 7
FLAGS, H0, U0, V0, OU0, OV0, OU1, OV1, ADJ = range(7, 16)
FIELDS = 16

STATIC = ("cov", "gr", "fri", "cce", "ccs", "de", "ds")
STEP = ("ce", "cs", "u1", "v1", "u2", "v2", "u3", "v3")
SWEEP = ("pe", "ps", "deu", "dev", "dsu", "dsv", "yu", "yv", "inv")
BACK = ("qu", "qv", "e", "bu", "bv")
REST = ("hce", "hcs", "hacc", "facc", "g1", "f1", "g0", "f0")


def scratch_names():
    names = list(STATIC)
    for n in range(2):
        names += [f"{n}{name}" for name in STEP]
        for j in range(3):
            names += [f"{n}{j}{name}" for name in SWEEP]
    for b in range(2):
        names += [f"b{b}{name}" for name in BACK]
    return names + list(REST)


NAMES = scratch_names()


def make_kernel(ny, nx, rows, cols, cell_count):
    strips = rows // 8
    total = strips + 2 * RIM
    first, last = RIM - 1, RIM + strips + 1
    width = cols + 128

    def kernel(
        thick_hbm, vel_hbm, slope_hbm, beta_hbm, mask_hbm, flags_hbm, obs_hbm, adj_hbm,
        beta_out, thick_out, misfit_out,
        fld, col_send, col_recv, row_send, row_recv, sum_x, sum_y, send_sem, recv_sem,
        sx_send, sx_recv, sy_send, sy_recv, in_sem,
        thick_in, vel_in, slope_in, beta_in, mask_in, flags_in, obs_in, adj_in, *refs,
    ):
        pairs = (
            (mask_hbm, mask_in), (beta_hbm, beta_in), (slope_hbm, slope_in), (thick_hbm, thick_in),
            (vel_hbm, vel_in), (flags_hbm, flags_in), (obs_hbm, obs_in), (adj_hbm, adj_in),
        )
        loads = [
            pltpu.make_async_copy(src, dst, in_sem.at[i]) for i, (src, dst) in enumerate(pairs)
        ]
        for load in loads:
            load.start()
        s = dict(zip(NAMES, refs))
        gy, gx = lax.axis_index("gy"), lax.axis_index("gx")
        centre = slice(RIM, RIM + strips)

        def exists(dy, dx):
            ok = None
            for move, at, count in ((dy, gy, ny), (dx, gx, nx)):
                if move:
                    here = at > 0 if move < 0 else at < count - 1
                    ok = here if ok is None else jnp.logical_and(ok, here)
            return ok

        diagonals = ((-1, -1), (-1, 1), (1, -1), (1, 1))
        sides = ((-1, 0), (1, 0), (0, -1), (0, 1))

        zero_rows = jnp.zeros((FIELDS, 2, 8, cols), jnp.float32)
        fld[:, 0:RIM, :, 0:cols] = zero_rows
        fld[:, RIM + strips : total, :, 0:cols] = zero_rows
        col_recv[...] = jnp.zeros_like(col_recv)
        row_recv[...] = jnp.zeros_like(row_recv)

        barrier = pltpu.get_barrier_semaphore()
        for off in range(1, nx):
            pl.semaphore_signal(
                barrier, inc=1, device_id=(gy, lax.rem(gx + off, nx)), device_id_type=MESH
            )
        for off in range(1, ny):
            pl.semaphore_signal(
                barrier, inc=1, device_id=(lax.rem(gy + off, ny), gx), device_id_type=MESH
            )
        for dy, dx in diagonals:

            @pl.when(exists(dy, dx))
            def _():
                pl.semaphore_signal(
                    barrier, inc=1, device_id=(gy + dy, gx + dx), device_id_type=MESH
                )

        def place(field, value):
            fld[field, centre, :, 0:cols] = value.astype(jnp.float32).reshape(strips, 8, cols)

        lane = lax.broadcasted_iota(jnp.int32, (8, 128), 1)
        sub = lax.broadcasted_iota(jnp.int32, (8, width), 0)
        sub_own = lax.broadcasted_iota(jnp.int32, (8, cols), 0)
        hi = RIM + strips

        for load in loads[:5]:
            load.wait()
        place(MASK, mask_in[...])
        place(BETA, beta_in[...])
        place(SLU, slope_in[0])
        place(SLV, slope_in[1])
        place(H1, thick_in[1])
        place(U1, vel_in[1, 0])
        place(V1, vel_in[1, 1])

        for up in range(2):
            at, row = (RIM + 1, 0) if up else (hi - 2, 6)
            for strip in range(2):
                packed = jnp.zeros((8, cols), jnp.float32)
                for i in range(min(4, DEEP - 4 * strip)):
                    x = fld[4 * strip + i, at, :, 0:cols]
                    move = (2 * i - row) % 8
                    if move:
                        x = pltpu.roll(x, move, 0)
                    inside = jnp.logical_and(sub_own >= 2 * i, sub_own < 2 * i + 2)
                    packed = jnp.where(inside, x, packed)
                row_send[up, strip] = packed

        beside = [
            jnp.where(at > 0, 1, 0) + jnp.where(at < count - 1, 1, 0)
            for at, count in ((gy, ny), (gx, nx))
        ]
        pl.semaphore_wait(barrier, (nx - 1) + (ny - 1) + beside[0] * beside[1])

        def begin(plan, base):
            copies = []
            for i, (dy, dx, src, dst) in enumerate(plan):
                copy = pltpu.make_async_remote_copy(
                    src_ref=src, dst_ref=dst,
                    send_sem=send_sem.at[base + i], recv_sem=recv_sem.at[base + i],
                    device_id=(gy + dy, gx + dx), device_id_type=MESH,
                )
                copies.append((dy, dx, copy))

                @pl.when(exists(dy, dx))
                def _():
                    copy.start()

            return copies

        def arrived(copies):
            for dy, dx, copy in copies:

                @pl.when(exists(-dy, -dx))
                def _():
                    copy.wait_recv()

        def row_plan(fields):
            return [
                (-1, 0, fld.at[fields, RIM, :, 0:cols], fld.at[fields, hi, :, 0:cols]),
                (1, 0, fld.at[fields, hi - 1, :, 0:cols], fld.at[fields, RIM - 1, :, 0:cols]),
            ]

        def col_plan(tile):
            send, recv = col_send.at[tile], col_recv.at[tile]
            plan = []
            for side, dx in ((0, -1), (1, 1)):
                plan.append((0, dx, send.at[side], recv.at[side, centre]))
                plan.append((-1, dx, send.at[side, 0:2], recv.at[side, hi : hi + 2]))
                plan.append((1, dx, send.at[side, strips - 2 : strips], recv.at[side, 0:2]))
            return plan

        per_tile = 128 // COLS

        def pack(tile):
            def pack_body(k, _):
                for side, at in ((0, 0), (1, cols - 128)):
                    packed = jnp.zeros((8, 128), jnp.float32)
                    for i in range(per_tile):
                        x = fld[tile * per_tile + i, k + RIM, :, at : at + 128]
                        move = (i * COLS - (0 if side == 0 else 128 - COLS)) % 128
                        if move:
                            x = pltpu.roll(x, move, 1)
                        inside = jnp.logical_and(lane >= i * COLS, lane < (i + 1) * COLS)
                        packed = jnp.where(inside, x, packed)
                    col_send[tile, side, k] = packed
                return 0

            lax.fori_loop(0, strips, pack_body, 0, unroll=2)

        def unpack(tile):
            def unpack_body(k, _):
                nxt, prv = col_recv[tile, 0, k], col_recv[tile, 1, k]
                for i in range(per_tile):
                    a = pltpu.roll(nxt, (-i * COLS) % 128, 1) if i else nxt
                    move = (128 - COLS - i * COLS) % 128
                    b = pltpu.roll(prv, move, 1) if move else prv
                    both = jnp.where(lane < COLS, a, jnp.where(lane >= 128 - COLS, b, 0.0))
                    fld[tile * per_tile + i, k, :, cols:width] = both
                return 0

            lax.fori_loop(0, total, unpack_body, 0, unroll=2)

        near = begin(
            row_plan(slice(0, DEEP))
            + [(-1, 0, row_send.at[1], row_recv.at[1]), (1, 0, row_send.at[0], row_recv.at[0])],
            0,
        )
        for load in loads[5:]:
            load.wait()
        place(FLAGS, flags_in[...])
        pack(0)
        near += begin(col_plan(0), 4)
        place(H0, thick_in[0])
        place(U0, vel_in[0, 0])
        place(V0, vel_in[0, 1])
        place(OU0, obs_in[0, 0])
        place(OV0, obs_in[0, 1])
        place(OU1, obs_in[1, 0])
        place(OV1, obs_in[1, 1])
        place(ADJ, adj_in[...])
        far = begin(row_plan(slice(DEEP, FIELDS)), 10)
        pack(1)
        far += begin(col_plan(1), 12)

        for n, (ou, ov) in enumerate(((OU0, OV0), (OU1, OV1))):
            def scale_body(k, acc, ou=ou, ov=ov):
                a, b = fld[ou, k, :, 0:cols], fld[ov, k, :, 0:cols]
                t = jnp.where(fld[MASK, k, :, 0:cols] == 2.0, a * a + b * b, 0.0)
                for c in range(0, cols, 128):
                    acc = acc + t[:, c : c + 128]
                return acc

            sum_x[0, 0, n] = lax.fori_loop(
                RIM, RIM + strips, scale_body, jnp.zeros((8, 128), jnp.float32), unroll=2
            )

        def spread(which, axis):
            buf, ssem, rsem, count = (
                (sum_x, sx_send, sx_recv, nx) if axis == "gx" else (sum_y, sy_send, sy_recv, ny)
            )
            made = []
            for off in range(1, count):
                peer = (
                    (gy, lax.rem(gx + off, nx)) if axis == "gx" else (lax.rem(gy + off, ny), gx)
                )
                made.append(
                    pltpu.make_async_remote_copy(
                        src_ref=buf.at[which, 0], dst_ref=buf.at[which, off],
                        send_sem=ssem.at[which, off], recv_sem=rsem.at[which, off],
                        device_id=peer, device_id_type=MESH,
                    )
                )
            return made

        def added(which, axis, n):
            buf, me, count = (sum_x, gx, nx) if axis == "gx" else (sum_y, gy, ny)
            acc = jnp.zeros((8, 128), jnp.float32)
            for src in range(count):
                acc = acc + buf[which, lax.rem(me - src + count, count), n]
            return acc

        def whole(tile):
            return jnp.sum(jnp.sum(tile, axis=1, keepdims=True), axis=0, keepdims=True)

        scale_x = spread(0, "gx")
        for copy in scale_x:
            copy.start()

        arrived(near)
        unpack(0)
        for up in range(2):
            at, row = (hi + 1, 0) if up else (0, 6)
            for strip in range(2):
                packed = row_recv[up, strip]
                for i in range(min(4, DEEP - 4 * strip)):
                    move = (row - 2 * i) % 8
                    x = pltpu.roll(packed, move, 0) if move else packed
                    inside = jnp.logical_and(sub_own >= row, sub_own < row + 2)
                    fld[4 * strip + i, at, :, 0:cols] = jnp.where(inside, x, 0.0)

        def east(x):
            return pltpu.roll(x, width - 1, 1)

        def west(x):
            return pltpu.roll(x, 1, 1)

        def south(cur, nxt):
            return pltpu.roll(jnp.where(sub == 0, nxt, cur), 7, 0)

        def north(prev, cur):
            return pltpu.roll(jnp.where(sub == 7, prev, cur), 1, 0)

        zero = jnp.zeros((8, width), jnp.float32)

        def after(k):
            return jnp.minimum(k + 1, total - 1)

        def static_body(k, _):
            mask = fld[MASK, k]
            cov = jnp.where(mask > 0.0, 1.0, 0.0)
            cov_n = jnp.where(fld[MASK, after(k)] > 0.0, 1.0, 0.0)
            gr = jnp.where(mask == 2.0, 1.0, 0.0)
            cce = 0.5 * cov * east(cov)
            ccs = 0.5 * cov * south(cov, cov_n)
            s["cov"][k] = cov
            s["gr"][k] = gr
            s["fri"][k] = fld[BETA, k] * gr
            s["cce"][k] = cce
            s["ccs"][k] = ccs
            h = fld[H1, k]
            s["1ce"][k] = cce * (h + east(h))
            s["1cs"][k] = ccs * (h + south(h, fld[H1, after(k)]))
            return 0

        lax.fori_loop(0, total, static_body, 0, unroll=2)

        def later_body(k, _):
            flags, h = fld[FLAGS, k], fld[H0, k]
            ds = jnp.where(flags >= 2.0, 1.0, 0.0)
            s["ds"][k] = ds
            s["de"][k] = flags - 2.0 * ds
            s["0ce"][k] = s["cce"][k] * (h + east(h))
            s["0cs"][k] = s["ccs"][k] * (h + south(h, fld[H0, k + 1]))
            return 0

        H = (H0, H1)
        W = ((U0, V0), (U1, V1))

        def velocity(n, j):
            if j == 0:
                return fld.at[W[n][0]], fld.at[W[n][1]]
            return s[f"{n}u{j}"], s[f"{n}v{j}"]

        def edge_zero(names):
            for name in names:
                for k in (first - 1, last):
                    s[name][k] = zero

        edge_zero([f"{n}{c}{j}" for n in range(2) for j in (1, 2, 3) for c in "uv"])
        edge_zero([f"b{b}{c}" for b in range(2) for c in ("qu", "qv", "e")] + ["g1"])

        def forward(n, j, lo, end):
            u_ref, v_ref = velocity(n, j)
            u_to, v_to = velocity(n, j + 1)
            t = {name: s[f"{n}{j}{name}"] for name in SWEEP}

            def body(k, carry):
                pfu, pfv, pc = carry
                kn = after(k)
                u, v = u_ref[k], v_ref[k]
                deu, dev = east(u) - u, east(v) - v
                dsu, dsv = south(u, u_ref[kn]) - u, south(v, v_ref[kn]) - v
                pe = jnp.exp(jnp.log(1.0 + (deu * deu + dev * dev)) * (-1.0 / 3.0))
                ps = jnp.exp(jnp.log(1.0 + (dsu * dsu + dsv * dsv)) * (-1.0 / 3.0))
                ce, cs = s[f"{n}ce"][k] * pe, s[f"{n}cs"][k] * ps
                feu, fev, fsu, fsv = ce * deu, ce * dev, cs * dsu, cs * dsv
                fri, h = s["fri"][k], fld[H[n], k]
                inv = 1.0 / (1.0 + fri + ((ce + west(ce)) + (cs + north(pc, cs))))
                ru = h * fld[SLU, k] - fri * u + ((feu - west(feu)) + (fsu - north(pfu, fsu)))
                rv = h * fld[SLV, k] - fri * v + ((fev - west(fev)) + (fsv - north(pfv, fsv)))
                yu, yv = ru * inv, rv * inv
                cov = s["cov"][k]
                u_to[k] = cov * (u + RELAXATION * yu)
                v_to[k] = cov * (v + RELAXATION * yv)
                for name, value in zip(SWEEP, (pe, ps, deu, dev, dsu, dsv, yu, yv, inv)):
                    t[name][k] = value
                return fsu, fsv, cs

            lax.fori_loop(lo, end, body, (zero, zero, zero), unroll=6 if end - lo == total else 5)

        forward(1, 0, 0, total)
        forward(1, 1, first, last)
        forward(1, 2, first, last)
        for copy in scale_x:
            copy.wait()
        for n in range(2):
            sum_y[0, 0, n] = added(0, "gx", n)
        scale_y = spread(0, "gy")
        for copy in scale_y:
            copy.start()
        arrived(far)
        unpack(1)
        lax.fori_loop(first, last, later_body, 0, unroll=2)
        forward(0, 0, first, last)
        forward(0, 1, first, last)
        forward(0, 2, first, last)

        O = ((OU0, OV0), (OU1, OV1))
        for n in range(2):
            def misfit_body(k, acc, n=n):
                a = s[f"{n}u3"][k, :, 0:cols] - fld[O[n][0], k, :, 0:cols]
                b = s[f"{n}v3"][k, :, 0:cols] - fld[O[n][1], k, :, 0:cols]
                t = s["gr"][k, :, 0:cols] * (a * a + b * b)
                for c in range(0, cols, 128):
                    acc = acc + t[:, c : c + 128]
                return acc

            sum_x[1, 0, n] = 0.5 * lax.fori_loop(
                RIM, RIM + strips, misfit_body, jnp.zeros((8, 128), jnp.float32), unroll=2
            )
        misfit_x = spread(1, "gx")
        for copy in misfit_x:
            copy.start()

        for copy in scale_y:
            copy.wait()
        scales = [whole(added(0, "gy", n)) * (1.0 / cell_count) + EPSILON for n in range(2)]

        def emit(n, j, b, k, lu, lv):
            cov, fri = s["cov"][k], s["fri"][k]
            au, av = cov * lu, cov * lv
            inv = RELAXATION * s[f"{n}{j}inv"][k]
            qu, qv = au * inv, av * inv
            s[f"b{b}qu"][k] = qu
            s[f"b{b}qv"][k] = qv
            s[f"b{b}e"][k] = -(qu * s[f"{n}{j}yu"][k] + qv * s[f"{n}{j}yv"][k])
            s[f"b{b}bu"][k] = au - fri * qu
            s[f"b{b}bv"][k] = av - fri * qv

        def transport(n, g_ref):
            per_scale = jnp.broadcast_to(1.0 / scales[n], (8, width))

            def body(k, carry):
                pvs, phs = carry
                kn = k + 1
                g, gn = s["cov"][k] * g_ref[k], s["cov"][kn] * g_ref[kn]
                h, hn = fld[H[n], k], fld[H[n], kn]
                u, v = s[f"{n}u3"][k], s[f"{n}v3"][k]
                de, ds = s["de"][k], s["ds"][k]
                pse = (TIME_STEP * s["cce"][k]) * (east(g) - g)
                pss = (TIME_STEP * s["ccs"][k]) * (south(g, gn) - g)
                ue = pse * (de * h + (1.0 - de) * east(h))
                vs = pss * (ds * h + (1.0 - ds) * south(h, hn))
                he = pse * (u + east(u))
                hs = pss * (v + south(v, s[f"{n}v3"][kn]))
                he_here, hs_here = de * he, ds * hs
                he_there, hs_there = he - he_here, hs - hs_here
                seed = s["gr"][k] * per_scale
                lu = seed * (u - fld[O[n][0], k]) + (ue + west(ue))
                lv = seed * (v - fld[O[n][1], k]) + (vs + north(pvs, vs))
                s["hacc"][k] = g + (he_here + west(he_there)) + (hs_here + north(phs, hs_there))
                emit(n, 2, 0, k, lu, lv)
                return vs, hs_there

            lax.fori_loop(first, last, body, (zero, zero), unroll=5)

        def backward(n, j, b, end, g_to=None, f_to=None):
            u_ref, v_ref = velocity(n, j)
            t = {name: s[f"{n}{j}{name}"] for name in SWEEP}
            q = {name: s[f"b{b}{name}"] for name in BACK}
            start, finish = j == 2, j == 0

            def body(k, carry):
                kn = k + 1
                qu, qv, e = q["qu"][k], q["qv"][k], q["e"][k]
                feu, fev = qu - east(qu), qv - east(qv)
                fsu, fsv = qu - south(qu, q["qu"][kn]), qv - south(qv, q["qv"][kn])
                pe, ps = t["pe"][k], t["ps"][k]
                deu, dev, dsu, dsv = t["deu"][k], t["dev"][k], t["dsu"][k], t["dsv"][k]
                ke = (feu * deu + fev * dev) + (e + east(e))
                ks = (fsu * dsu + fsv * dsv) + (e + south(e, q["e"][kn]))
                kpe, kps = ke * pe, ks * ps
                f = e - (qu * u_ref[k] + qv * v_ref[k])
                h = qu * fld[SLU, k] + qv * fld[SLV, k] + s["hacc"][k]
                if not start:
                    kpe_sum, kps_sum = s["hce"][k] + kpe, s["hcs"][k] + kps
                    f = f + s["facc"][k]
                else:
                    kpe_sum, kps_sum = kpe, kps
                if finish:
                    ge, gs = s["cce"][k] * kpe_sum, s["ccs"][k] * kps_sum
                    g_to[k] = h + ((ge + west(ge)) + (gs + north(carry[0], gs)))
                    f_to[k] = f
                    return (gs,)
                s["hce"][k] = kpe_sum
                s["hcs"][k] = kps_sum
                s["facc"][k] = f
                s["hacc"][k] = h
                ce, cs = s[f"{n}ce"][k] * pe, s[f"{n}cs"][k] * ps
                te = (2.0 / 3.0) * ce * (pe * pe) * kpe
                ts = (2.0 / 3.0) * cs * (ps * ps) * kps
                xeu, xev = ce * feu - te * deu, ce * fev - te * dev
                xsu, xsv = cs * fsu - ts * dsu, cs * fsv - ts * dsv
                lu = q["bu"][k] + ((west(xeu) - xeu) + (north(carry[0], xsu) - xsu))
                lv = q["bv"][k] + ((west(xev) - xev) + (north(carry[1], xsv) - xsv))
                emit(n, j - 1, 1 - b, k, lu, lv)
                return xsu, xsv

            lax.fori_loop(first, end, body, (zero,) if finish else (zero, zero), unroll=5)

        transport(1, fld.at[ADJ])
        backward(1, 2, 0, last)
        backward(1, 1, 1, last)
        backward(1, 0, 0, last, s["g1"], s["f1"])

        for copy in misfit_x:
            copy.wait()
        for n in range(2):
            sum_y[1, 0, n] = added(1, "gx", n)
        misfit_y = spread(1, "gy")
        for copy in misfit_y:
            copy.start()

        transport(0, s["g1"])
        backward(0, 2, 0, last)
        backward(0, 1, 1, last)
        backward(0, 0, 0, last, s["g0"], s["f0"])

        f_sum = s["f1"][centre, :, 0:cols] + s["f0"][centre, :, 0:cols]
        beta_out[...] = s["gr"][centre, :, 0:cols] * f_sum
        thick_out[...] = s["g0"][centre, :, 0:cols]

        for copy in misfit_y:
            copy.wait()
        parts = [whole(added(1, "gy", n)) * (1.0 / cell_count) / scales[n] for n in range(2)]
        misfit_out[...] = parts[1] + parts[0]
        for dy, dx, copy in near + far:

            @pl.when(exists(dy, dx))
            def _():
                copy.wait_send()

    return kernel


def on_device(*args):
    ny, nx = lax.axis_size("gy"), lax.axis_size("gx")
    rows, cols = args[3].shape
    strips = rows // 8
    total = strips + 2 * RIM
    width = cols + 128
    vmem = pl.BlockSpec(memory_space=pltpu.VMEM)
    dma = pltpu.SemaphoreType.DMA
    beta, thick, misfit = pl.pallas_call(
        make_kernel(ny, nx, rows, cols, rows * cols * ny * nx),
        out_shape=(
            jax.ShapeDtypeStruct((strips, 8, cols), jnp.float32),
            jax.ShapeDtypeStruct((strips, 8, cols), jnp.float32),
            jax.ShapeDtypeStruct((1, 1), jnp.float32),
        ),
        in_specs=[pl.BlockSpec(memory_space=pltpu.HBM)] * len(args),
        out_specs=(vmem, vmem, vmem),
        scratch_shapes=[
            pltpu.VMEM((FIELDS, total, 8, width), jnp.float32),
            pltpu.VMEM((FIELDS * COLS // 128, 2, strips, 8, 128), jnp.float32),
            pltpu.VMEM((FIELDS * COLS // 128, 2, total, 8, 128), jnp.float32),
            pltpu.VMEM((2, 2, 8, cols), jnp.float32),
            pltpu.VMEM((2, 2, 8, cols), jnp.float32),
            pltpu.VMEM((2, nx, 2, 8, 128), jnp.float32),
            pltpu.VMEM((2, ny, 2, 8, 128), jnp.float32),
            dma((18,)), dma((18,)),
            dma((2, nx)), dma((2, nx)), dma((2, ny)), dma((2, ny)), dma((len(args),)),
        ]
        + [pltpu.VMEM(arg.shape, arg.dtype) for arg in args]
        + [pltpu.VMEM((total, 8, width), jnp.float32)] * len(NAMES),
        compiler_params=pltpu.CompilerParams(
            collective_id=0, has_side_effects=True, vmem_limit_bytes=62 * 1024 * 1024
        ),
    )(*args)
    return beta.reshape(rows, cols), thick.reshape(rows, cols), misfit.reshape(())


def solution(mesh):
    in_specs = (
        P(None, "gy", "gx"),
        P(None, None, "gy", "gx"),
        P(None, "gy", "gx"),
        P("gy", "gx"),
        P("gy", "gx"),
        P("gy", "gx"),
        P(None, None, "gy", "gx"),
        P("gy", "gx"),
    )
    out_specs = (P("gy", "gx"), P("gy", "gx"), P())
    return jax.shard_map(
        on_device, mesh=mesh, in_specs=in_specs, out_specs=out_specs, check_vma=False
    )
```

```python
import jax
import jax.numpy as jnp
from jax import lax
from jax.experimental import pallas as pl
from jax.experimental.pallas import tpu as pltpu
from jax.sharding import PartitionSpec as P

RELAXATION = 0.8
TIME_STEP = 0.1
EPSILON = 1e-06
MESH = pl.DeviceIdType.MESH

RIM = 2
COLS = 16

MASK, BETA, SLU, SLV, H1, U1, V1 = range(7)
DEEP = 7
FLAGS, H0, U0, V0, OU0, OV0, OU1, OV1, ADJ = range(7, 16)
FIELDS = 16

STATIC = ("cov", "gr", "fri", "cce", "ccs", "de", "ds")
STEP = ("ce", "cs", "u1", "v1", "u2", "v2", "u3", "v3")
SWEEP = ("pe", "ps", "deu", "dev", "dsu", "dsv", "yu", "yv", "inv")
BACK = ("qu", "qv", "e", "bu", "bv")
REST = ("hce", "hcs", "hacc", "facc", "g1", "f1", "g0", "f0")


def scratch_names():
    names = list(STATIC)
    for n in range(2):
        names += [f"{n}{name}" for name in STEP]
        for j in range(3):
            names += [f"{n}{j}{name}" for name in SWEEP]
    for b in range(2):
        names += [f"b{b}{name}" for name in BACK]
    return names + list(REST)


NAMES = scratch_names()


def make_kernel(ny, nx, rows, cols, cell_count):
    strips = rows // 8
    total = strips + 2 * RIM
    first, last = RIM - 1, RIM + strips + 1
    width = cols + 128

    def kernel(
        thick_hbm, vel_hbm, slope_hbm, beta_hbm, mask_hbm, flags_hbm, obs_hbm, adj_hbm,
        beta_out, thick_out, misfit_out,
        fld, col_send, col_recv, row_send, row_recv, sum_x, sum_y, send_sem, recv_sem,
        sx_send, sx_recv, sy_send, sy_recv, in_sem,
        thick_in, vel_in, slope_in, beta_in, mask_in, flags_in, obs_in, adj_in, *refs,
    ):
        pairs = (
            (mask_hbm, mask_in), (beta_hbm, beta_in), (slope_hbm, slope_in), (thick_hbm, thick_in),
            (vel_hbm, vel_in), (flags_hbm, flags_in), (obs_hbm, obs_in), (adj_hbm, adj_in),
        )
        loads = [
            pltpu.make_async_copy(src, dst, in_sem.at[i]) for i, (src, dst) in enumerate(pairs)
        ]
        for load in loads:
            load.start()
        s = dict(zip(NAMES, refs))
        gy, gx = lax.axis_index("gy"), lax.axis_index("gx")
        centre = slice(RIM, RIM + strips)

        def exists(dy, dx):
            ok = None
            for move, at, count in ((dy, gy, ny), (dx, gx, nx)):
                if move:
                    here = at > 0 if move < 0 else at < count - 1
                    ok = here if ok is None else jnp.logical_and(ok, here)
            return ok

        diagonals = ((-1, -1), (-1, 1), (1, -1), (1, 1))
        sides = ((-1, 0), (1, 0), (0, -1), (0, 1))

        zero_rows = jnp.zeros((FIELDS, 2, 8, cols), jnp.float32)
        fld[:, 0:RIM, :, 0:cols] = zero_rows
        fld[:, RIM + strips : total, :, 0:cols] = zero_rows
        col_recv[...] = jnp.zeros_like(col_recv)
        row_recv[...] = jnp.zeros_like(row_recv)

        barrier = pltpu.get_barrier_semaphore()
        for off in range(1, nx):
            pl.semaphore_signal(
                barrier, inc=1, device_id=(gy, lax.rem(gx + off, nx)), device_id_type=MESH
            )
        for off in range(1, ny):
            pl.semaphore_signal(
                barrier, inc=1, device_id=(lax.rem(gy + off, ny), gx), device_id_type=MESH
            )
        for dy, dx in diagonals:

            @pl.when(exists(dy, dx))
            def _():
                pl.semaphore_signal(
                    barrier, inc=1, device_id=(gy + dy, gx + dx), device_id_type=MESH
                )

        def place(field, value):
            fld[field, centre, :, 0:cols] = value.astype(jnp.float32).reshape(strips, 8, cols)

        lane = lax.broadcasted_iota(jnp.int32, (8, 128), 1)
        sub = lax.broadcasted_iota(jnp.int32, (8, width), 0)
        sub_own = lax.broadcasted_iota(jnp.int32, (8, cols), 0)
        hi = RIM + strips

        for load in loads[:5]:
            load.wait()
        place(MASK, mask_in[...])
        place(BETA, beta_in[...])
        place(SLU, slope_in[0])
        place(SLV, slope_in[1])
        place(H1, thick_in[1])
        place(U1, vel_in[1, 0])
        place(V1, vel_in[1, 1])

        for up in range(2):
            at, row = (RIM + 1, 0) if up else (hi - 2, 6)
            for strip in range(2):
                packed = jnp.zeros((8, cols), jnp.float32)
                for i in range(min(4, DEEP - 4 * strip)):
                    x = fld[4 * strip + i, at, :, 0:cols]
                    move = (2 * i - row) % 8
                    if move:
                        x = pltpu.roll(x, move, 0)
                    inside = jnp.logical_and(sub_own >= 2 * i, sub_own < 2 * i + 2)
                    packed = jnp.where(inside, x, packed)
                row_send[up, strip] = packed

        def begin(plan, base):
            copies = []
            for i, (dy, dx, src, dst) in enumerate(plan):
                copy = pltpu.make_async_remote_copy(
                    src_ref=src, dst_ref=dst,
                    send_sem=send_sem.at[base + i], recv_sem=recv_sem.at[base + i],
                    device_id=(gy + dy, gx + dx), device_id_type=MESH,
                )
                copies.append((dy, dx, copy))

                @pl.when(exists(dy, dx))
                def _():
                    copy.start()

            return copies

        def arrived(copies):
            for dy, dx, copy in copies:

                @pl.when(exists(-dy, -dx))
                def _():
                    copy.wait_recv()

        def row_plan(fields):
            return [
                (-1, 0, fld.at[fields, RIM, :, 0:cols], fld.at[fields, hi, :, 0:cols]),
                (1, 0, fld.at[fields, hi - 1, :, 0:cols], fld.at[fields, RIM - 1, :, 0:cols]),
            ]

        def col_plan(tile):
            send, recv = col_send.at[tile], col_recv.at[tile]
            plan = []
            for side, dx in ((0, -1), (1, 1)):
                plan.append((0, dx, send.at[side], recv.at[side, centre]))
                plan.append((-1, dx, send.at[side, 0:2], recv.at[side, hi : hi + 2]))
                plan.append((1, dx, send.at[side, strips - 2 : strips], recv.at[side, 0:2]))
            return plan

        per_tile = 128 // COLS

        def pack(tile):
            def pack_body(k, _):
                for side, at in ((0, 0), (1, cols - 128)):
                    packed = jnp.zeros((8, 128), jnp.float32)
                    for i in range(per_tile):
                        x = fld[tile * per_tile + i, k + RIM, :, at : at + 128]
                        move = (i * COLS - (0 if side == 0 else 128 - COLS)) % 128
                        if move:
                            x = pltpu.roll(x, move, 1)
                        inside = jnp.logical_and(lane >= i * COLS, lane < (i + 1) * COLS)
                        packed = jnp.where(inside, x, packed)
                    col_send[tile, side, k] = packed
                return 0

            lax.fori_loop(0, strips, pack_body, 0, unroll=2)

        def unpack(tile):
            def unpack_body(k, _):
                nxt, prv = col_recv[tile, 0, k], col_recv[tile, 1, k]
                for i in range(per_tile):
                    a = pltpu.roll(nxt, (-i * COLS) % 128, 1) if i else nxt
                    move = (128 - COLS - i * COLS) % 128
                    b = pltpu.roll(prv, move, 1) if move else prv
                    both = jnp.where(lane < COLS, a, jnp.where(lane >= 128 - COLS, b, 0.0))
                    fld[tile * per_tile + i, k, :, cols:width] = both
                return 0

            lax.fori_loop(0, total, unpack_body, 0, unroll=2)

        def spread(which, axis):
            buf, ssem, rsem, count = (
                (sum_x, sx_send, sx_recv, nx) if axis == "gx" else (sum_y, sy_send, sy_recv, ny)
            )
            made = []
            for off in range(1, count):
                peer = (
                    (gy, lax.rem(gx + off, nx)) if axis == "gx" else (lax.rem(gy + off, ny), gx)
                )
                made.append(
                    pltpu.make_async_remote_copy(
                        src_ref=buf.at[which, 0], dst_ref=buf.at[which, off],
                        send_sem=ssem.at[which, off], recv_sem=rsem.at[which, off],
                        device_id=peer, device_id_type=MESH,
                    )
                )
            return made

        def added(which, axis, n):
            buf, me, count = (sum_x, gx, nx) if axis == "gx" else (sum_y, gy, ny)
            acc = jnp.zeros((8, 128), jnp.float32)
            for src in range(count):
                acc = acc + buf[which, lax.rem(me - src + count, count), n]
            return acc

        def whole(tile):
            return jnp.sum(jnp.sum(tile, axis=1, keepdims=True), axis=0, keepdims=True)

        for load in loads[5:]:
            load.wait()
        place(FLAGS, flags_in[...])
        place(H0, thick_in[0])
        place(U0, vel_in[0, 0])
        place(V0, vel_in[0, 1])
        place(OU0, obs_in[0, 0])
        place(OV0, obs_in[0, 1])
        place(OU1, obs_in[1, 0])
        place(OV1, obs_in[1, 1])
        place(ADJ, adj_in[...])
        pack(0)
        for n, (ou, ov) in enumerate(((OU0, OV0), (OU1, OV1))):
            def scale_body(k, acc, ou=ou, ov=ov):
                a, b = fld[ou, k, :, 0:cols], fld[ov, k, :, 0:cols]
                t = jnp.where(fld[MASK, k, :, 0:cols] == 2.0, a * a + b * b, 0.0)
                for c in range(0, cols, 128):
                    acc = acc + t[:, c : c + 128]
                return acc

            sum_x[0, 0, n] = lax.fori_loop(
                RIM, RIM + strips, scale_body, jnp.zeros((8, 128), jnp.float32), unroll=2
            )

        pack(1)
        beside = [
            jnp.where(at > 0, 1, 0) + jnp.where(at < count - 1, 1, 0)
            for at, count in ((gy, ny), (gx, nx))
        ]
        pl.semaphore_wait(barrier, (nx - 1) + (ny - 1) + beside[0] * beside[1])

        near = begin(
            row_plan(slice(0, DEEP))
            + [(-1, 0, row_send.at[1], row_recv.at[1]), (1, 0, row_send.at[0], row_recv.at[0])],
            0,
        )
        near += begin(col_plan(0), 4)
        scale_x = spread(0, "gx")
        for copy in scale_x:
            copy.start()

        far = begin(row_plan(slice(DEEP, FIELDS)), 10)
        far += begin(col_plan(1), 12)

        arrived(near)
        unpack(0)
        for up in range(2):
            at, row = (hi + 1, 0) if up else (0, 6)
            for strip in range(2):
                packed = row_recv[up, strip]
                for i in range(min(4, DEEP - 4 * strip)):
                    move = (row - 2 * i) % 8
                    x = pltpu.roll(packed, move, 0) if move else packed
                    inside = jnp.logical_and(sub_own >= row, sub_own < row + 2)
                    fld[4 * strip + i, at, :, 0:cols] = jnp.where(inside, x, 0.0)

        for copy in scale_x:
            copy.wait()
        for n in range(2):
            sum_y[0, 0, n] = added(0, "gx", n)
        scale_y = spread(0, "gy")
        for copy in scale_y:
            copy.start()

        def east(x):
            return pltpu.roll(x, width - 1, 1)

        def west(x):
            return pltpu.roll(x, 1, 1)

        def south(cur, nxt):
            return pltpu.roll(jnp.where(sub == 0, nxt, cur), 7, 0)

        def north(prev, cur):
            return pltpu.roll(jnp.where(sub == 7, prev, cur), 1, 0)

        zero = jnp.zeros((8, width), jnp.float32)

        def after(k):
            return jnp.minimum(k + 1, total - 1)

        def static_body(k, _):
            mask = fld[MASK, k]
            cov = jnp.where(mask > 0.0, 1.0, 0.0)
            cov_n = jnp.where(fld[MASK, after(k)] > 0.0, 1.0, 0.0)
            gr = jnp.where(mask == 2.0, 1.0, 0.0)
            cce = 0.5 * cov * east(cov)
            ccs = 0.5 * cov * south(cov, cov_n)
            s["cov"][k] = cov
            s["gr"][k] = gr
            s["fri"][k] = fld[BETA, k] * gr
            s["cce"][k] = cce
            s["ccs"][k] = ccs
            h = fld[H1, k]
            s["1ce"][k] = cce * (h + east(h))
            s["1cs"][k] = ccs * (h + south(h, fld[H1, after(k)]))
            return 0

        lax.fori_loop(0, total, static_body, 0, unroll=2)

        def later_body(k, _):
            flags, h = fld[FLAGS, k], fld[H0, k]
            ds = jnp.where(flags >= 2.0, 1.0, 0.0)
            s["ds"][k] = ds
            s["de"][k] = flags - 2.0 * ds
            s["0ce"][k] = s["cce"][k] * (h + east(h))
            s["0cs"][k] = s["ccs"][k] * (h + south(h, fld[H0, k + 1]))
            return 0

        H = (H0, H1)
        W = ((U0, V0), (U1, V1))

        def velocity(n, j):
            if j == 0:
                return fld.at[W[n][0]], fld.at[W[n][1]]
            return s[f"{n}u{j}"], s[f"{n}v{j}"]

        def edge_zero(names):
            for name in names:
                for k in (first - 1, last):
                    s[name][k] = zero

        edge_zero([f"{n}{c}{j}" for n in range(2) for j in (1, 2, 3) for c in "uv"])
        edge_zero([f"b{b}{c}" for b in range(2) for c in ("qu", "qv", "e")] + ["g1"])

        def forward(n, j, lo, end):
            u_ref, v_ref = velocity(n, j)
            u_to, v_to = velocity(n, j + 1)
            t = {name: s[f"{n}{j}{name}"] for name in SWEEP}

            def body(k, carry):
                pfu, pfv, pc = carry
                kn = after(k)
                u, v = u_ref[k], v_ref[k]
                deu, dev = east(u) - u, east(v) - v
                dsu, dsv = south(u, u_ref[kn]) - u, south(v, v_ref[kn]) - v
                pe = jnp.exp(jnp.log(1.0 + (deu * deu + dev * dev)) * (-1.0 / 3.0))
                ps = jnp.exp(jnp.log(1.0 + (dsu * dsu + dsv * dsv)) * (-1.0 / 3.0))
                ce, cs = s[f"{n}ce"][k] * pe, s[f"{n}cs"][k] * ps
                feu, fev, fsu, fsv = ce * deu, ce * dev, cs * dsu, cs * dsv
                fri, h = s["fri"][k], fld[H[n], k]
                inv = 1.0 / (1.0 + fri + ((ce + west(ce)) + (cs + north(pc, cs))))
                ru = h * fld[SLU, k] - fri * u + ((feu - west(feu)) + (fsu - north(pfu, fsu)))
                rv = h * fld[SLV, k] - fri * v + ((fev - west(fev)) + (fsv - north(pfv, fsv)))
                yu, yv = ru * inv, rv * inv
                cov = s["cov"][k]
                u_to[k] = cov * (u + RELAXATION * yu)
                v_to[k] = cov * (v + RELAXATION * yv)
                for name, value in zip(SWEEP, (pe, ps, deu, dev, dsu, dsv, yu, yv, inv)):
                    t[name][k] = value
                return fsu, fsv, cs

            lax.fori_loop(lo, end, body, (zero, zero, zero), unroll=6 if end - lo == total else 5)

        forward(1, 0, 0, total)
        forward(1, 1, first, last)
        forward(1, 2, first, last)
        arrived(far)
        unpack(1)
        lax.fori_loop(first, last, later_body, 0, unroll=2)
        forward(0, 0, first, last)
        forward(0, 1, first, last)
        forward(0, 2, first, last)

        O = ((OU0, OV0), (OU1, OV1))
        for n in range(2):
            def misfit_body(k, acc, n=n):
                a = s[f"{n}u3"][k, :, 0:cols] - fld[O[n][0], k, :, 0:cols]
                b = s[f"{n}v3"][k, :, 0:cols] - fld[O[n][1], k, :, 0:cols]
                t = s["gr"][k, :, 0:cols] * (a * a + b * b)
                for c in range(0, cols, 128):
                    acc = acc + t[:, c : c + 128]
                return acc

            sum_x[1, 0, n] = 0.5 * lax.fori_loop(
                RIM, RIM + strips, misfit_body, jnp.zeros((8, 128), jnp.float32), unroll=2
            )
        misfit_x = spread(1, "gx")
        for copy in misfit_x:
            copy.start()

        for copy in scale_y:
            copy.wait()
        scales = [whole(added(0, "gy", n)) * (1.0 / cell_count) + EPSILON for n in range(2)]

        def emit(n, j, b, k, lu, lv):
            cov, fri = s["cov"][k], s["fri"][k]
            au, av = cov * lu, cov * lv
            inv = RELAXATION * s[f"{n}{j}inv"][k]
            qu, qv = au * inv, av * inv
            s[f"b{b}qu"][k] = qu
            s[f"b{b}qv"][k] = qv
            s[f"b{b}e"][k] = -(qu * s[f"{n}{j}yu"][k] + qv * s[f"{n}{j}yv"][k])
            s[f"b{b}bu"][k] = au - fri * qu
            s[f"b{b}bv"][k] = av - fri * qv

        def transport(n, g_ref):
            per_scale = jnp.broadcast_to(1.0 / scales[n], (8, width))

            def body(k, carry):
                pvs, phs = carry
                kn = k + 1
                g, gn = s["cov"][k] * g_ref[k], s["cov"][kn] * g_ref[kn]
                h, hn = fld[H[n], k], fld[H[n], kn]
                u, v = s[f"{n}u3"][k], s[f"{n}v3"][k]
                de, ds = s["de"][k], s["ds"][k]
                pse = (TIME_STEP * s["cce"][k]) * (east(g) - g)
                pss = (TIME_STEP * s["ccs"][k]) * (south(g, gn) - g)
                ue = pse * (de * h + (1.0 - de) * east(h))
                vs = pss * (ds * h + (1.0 - ds) * south(h, hn))
                he = pse * (u + east(u))
                hs = pss * (v + south(v, s[f"{n}v3"][kn]))
                he_here, hs_here = de * he, ds * hs
                he_there, hs_there = he - he_here, hs - hs_here
                seed = s["gr"][k] * per_scale
                lu = seed * (u - fld[O[n][0], k]) + (ue + west(ue))
                lv = seed * (v - fld[O[n][1], k]) + (vs + north(pvs, vs))
                s["hacc"][k] = g + (he_here + west(he_there)) + (hs_here + north(phs, hs_there))
                emit(n, 2, 0, k, lu, lv)
                return vs, hs_there

            lax.fori_loop(first, last, body, (zero, zero), unroll=5)

        def backward(n, j, b, end, g_to=None, f_to=None):
            u_ref, v_ref = velocity(n, j)
            t = {name: s[f"{n}{j}{name}"] for name in SWEEP}
            q = {name: s[f"b{b}{name}"] for name in BACK}
            start, finish = j == 2, j == 0

            def body(k, carry):
                kn = k + 1
                qu, qv, e = q["qu"][k], q["qv"][k], q["e"][k]
                feu, fev = qu - east(qu), qv - east(qv)
                fsu, fsv = qu - south(qu, q["qu"][kn]), qv - south(qv, q["qv"][kn])
                pe, ps = t["pe"][k], t["ps"][k]
                deu, dev, dsu, dsv = t["deu"][k], t["dev"][k], t["dsu"][k], t["dsv"][k]
                ke = (feu * deu + fev * dev) + (e + east(e))
                ks = (fsu * dsu + fsv * dsv) + (e + south(e, q["e"][kn]))
                kpe, kps = ke * pe, ks * ps
                f = e - (qu * u_ref[k] + qv * v_ref[k])
                h = qu * fld[SLU, k] + qv * fld[SLV, k] + s["hacc"][k]
                if not start:
                    kpe_sum, kps_sum = s["hce"][k] + kpe, s["hcs"][k] + kps
                    f = f + s["facc"][k]
                else:
                    kpe_sum, kps_sum = kpe, kps
                if finish:
                    ge, gs = s["cce"][k] * kpe_sum, s["ccs"][k] * kps_sum
                    g_to[k] = h + ((ge + west(ge)) + (gs + north(carry[0], gs)))
                    f_to[k] = f
                    return (gs,)
                s["hce"][k] = kpe_sum
                s["hcs"][k] = kps_sum
                s["facc"][k] = f
                s["hacc"][k] = h
                ce, cs = s[f"{n}ce"][k] * pe, s[f"{n}cs"][k] * ps
                te = (2.0 / 3.0) * ce * (pe * pe) * kpe
                ts = (2.0 / 3.0) * cs * (ps * ps) * kps
                xeu, xev = ce * feu - te * deu, ce * fev - te * dev
                xsu, xsv = cs * fsu - ts * dsu, cs * fsv - ts * dsv
                lu = q["bu"][k] + ((west(xeu) - xeu) + (north(carry[0], xsu) - xsu))
                lv = q["bv"][k] + ((west(xev) - xev) + (north(carry[1], xsv) - xsv))
                emit(n, j - 1, 1 - b, k, lu, lv)
                return xsu, xsv

            lax.fori_loop(first, end, body, (zero,) if finish else (zero, zero), unroll=5)

        transport(1, fld.at[ADJ])
        backward(1, 2, 0, last)
        backward(1, 1, 1, last)
        backward(1, 0, 0, last, s["g1"], s["f1"])

        for copy in misfit_x:
            copy.wait()
        for n in range(2):
            sum_y[1, 0, n] = added(1, "gx", n)
        misfit_y = spread(1, "gy")
        for copy in misfit_y:
            copy.start()

        transport(0, s["g1"])
        backward(0, 2, 0, last)
        backward(0, 1, 1, last)
        backward(0, 0, 0, last, s["g0"], s["f0"])

        f_sum = s["f1"][centre, :, 0:cols] + s["f0"][centre, :, 0:cols]
        beta_out[...] = s["gr"][centre, :, 0:cols] * f_sum
        thick_out[...] = s["g0"][centre, :, 0:cols]

        for copy in misfit_y:
            copy.wait()
        parts = [whole(added(1, "gy", n)) * (1.0 / cell_count) / scales[n] for n in range(2)]
        misfit_out[...] = parts[1] + parts[0]
        for dy, dx, copy in near + far:

            @pl.when(exists(dy, dx))
            def _():
                copy.wait_send()

    return kernel


def on_device(*args):
    ny, nx = lax.axis_size("gy"), lax.axis_size("gx")
    rows, cols = args[3].shape
    strips = rows // 8
    total = strips + 2 * RIM
    width = cols + 128
    vmem = pl.BlockSpec(memory_space=pltpu.VMEM)
    dma = pltpu.SemaphoreType.DMA
    beta, thick, misfit = pl.pallas_call(
        make_kernel(ny, nx, rows, cols, rows * cols * ny * nx),
        out_shape=(
            pltpu.VMEM((strips, 8, cols), jnp.float32),
            pltpu.VMEM((strips, 8, cols), jnp.float32),
            jax.ShapeDtypeStruct((1, 1), jnp.float32),
        ),
        in_specs=[pl.BlockSpec(memory_space=pltpu.HBM)] * len(args),
        out_specs=(vmem, vmem, vmem),
        scratch_shapes=[
            pltpu.VMEM((FIELDS, total, 8, width), jnp.float32),
            pltpu.VMEM((FIELDS * COLS // 128, 2, strips, 8, 128), jnp.float32),
            pltpu.VMEM((FIELDS * COLS // 128, 2, total, 8, 128), jnp.float32),
            pltpu.VMEM((2, 2, 8, cols), jnp.float32),
            pltpu.VMEM((2, 2, 8, cols), jnp.float32),
            pltpu.VMEM((2, nx, 2, 8, 128), jnp.float32),
            pltpu.VMEM((2, ny, 2, 8, 128), jnp.float32),
            dma((18,)), dma((18,)),
            dma((2, nx)), dma((2, nx)), dma((2, ny)), dma((2, ny)), dma((len(args),)),
        ]
        + [pltpu.VMEM(arg.shape, arg.dtype) for arg in args]
        + [pltpu.VMEM((total, 8, width), jnp.float32)] * len(NAMES),
        compiler_params=pltpu.CompilerParams(
            collective_id=0, has_side_effects=True, vmem_limit_bytes=62 * 1024 * 1024
        ),
    )(*args)
    return beta.reshape(rows, cols), thick.reshape(rows, cols), misfit.reshape(())


def solution(mesh):
    in_specs = (
        P(None, "gy", "gx"),
        P(None, None, "gy", "gx"),
        P(None, "gy", "gx"),
        P("gy", "gx"),
        P("gy", "gx"),
        P("gy", "gx"),
        P(None, None, "gy", "gx"),
        P("gy", "gx"),
    )
    out_specs = (P("gy", "gx"), P("gy", "gx"), P())
    return jax.shard_map(
        on_device, mesh=mesh, in_specs=in_specs, out_specs=out_specs, check_vma=False
    )
```

```python
import jax
import jax.numpy as jnp
from jax import lax
from jax.experimental import pallas as pl
from jax.experimental.pallas import tpu as pltpu
from jax.sharding import PartitionSpec as P

RELAXATION = 0.8
TIME_STEP = 0.1
EPSILON = 1e-06
MESH = pl.DeviceIdType.MESH

RIM = 2
COLS = 16

MASK, BETA, SLU, SLV, H1, U1, V1 = range(7)
DEEP = 7
FLAGS, H0, U0, V0, OU0, OV0, OU1, OV1, ADJ = range(7, 16)
FIELDS = 16

STATIC = ("cov", "gr", "fri", "cce", "ccs", "de", "ds")
STEP = ("ce", "cs", "u1", "v1", "u2", "v2", "u3", "v3")
SWEEP = ("pe", "ps", "deu", "dev", "dsu", "dsv", "yu", "yv", "inv")
BACK = ("qu", "qv", "e", "bu", "bv")
REST = ("hce", "hcs", "hacc", "facc", "g1", "f1", "g0", "f0")


def scratch_names():
    names = list(STATIC)
    for n in range(2):
        names += [f"{n}{name}" for name in STEP]
        for j in range(3):
            names += [f"{n}{j}{name}" for name in SWEEP]
    for b in range(2):
        names += [f"b{b}{name}" for name in BACK]
    return names + list(REST)


NAMES = scratch_names()


def make_kernel(ny, nx, rows, cols, cell_count):
    strips = rows // 8
    total = strips + 2 * RIM
    first, last = RIM - 1, RIM + strips + 1
    width = cols + 128

    def kernel(
        thick_hbm, vel_hbm, slope_hbm, beta_hbm, mask_hbm, flags_hbm, obs_hbm, adj_hbm,
        beta_out, thick_out, misfit_out,
        fld, col_send, col_recv, row_send, row_recv, sum_x, sum_y, send_sem, recv_sem,
        sx_send, sx_recv, sy_send, sy_recv, in_sem,
        thick_in, vel_in, slope_in, beta_in, mask_in, flags_in, obs_in, adj_in, *refs,
    ):
        pairs = (
            (mask_hbm, mask_in), (beta_hbm, beta_in), (slope_hbm, slope_in), (thick_hbm, thick_in),
            (vel_hbm, vel_in), (flags_hbm, flags_in), (obs_hbm, obs_in), (adj_hbm, adj_in),
        )
        loads = [
            pltpu.make_async_copy(src, dst, in_sem.at[i]) for i, (src, dst) in enumerate(pairs)
        ]
        for load in loads:
            load.start()
        s = dict(zip(NAMES, refs))
        gy, gx = lax.axis_index("gy"), lax.axis_index("gx")
        centre = slice(RIM, RIM + strips)

        def exists(dy, dx):
            ok = None
            for move, at, count in ((dy, gy, ny), (dx, gx, nx)):
                if move:
                    here = at > 0 if move < 0 else at < count - 1
                    ok = here if ok is None else jnp.logical_and(ok, here)
            return ok

        diagonals = ((-1, -1), (-1, 1), (1, -1), (1, 1))
        sides = ((-1, 0), (1, 0), (0, -1), (0, 1))

        zero_rows = jnp.zeros((FIELDS, 2, 8, cols), jnp.float32)
        fld[:, 0:RIM, :, 0:cols] = zero_rows
        fld[:, RIM + strips : total, :, 0:cols] = zero_rows
        col_recv[...] = jnp.zeros_like(col_recv)
        row_recv[...] = jnp.zeros_like(row_recv)

        barrier = pltpu.get_barrier_semaphore()
        for off in range(1, nx):
            pl.semaphore_signal(
                barrier, inc=1, device_id=(gy, lax.rem(gx + off, nx)), device_id_type=MESH
            )
        for off in range(1, ny):
            pl.semaphore_signal(
                barrier, inc=1, device_id=(lax.rem(gy + off, ny), gx), device_id_type=MESH
            )
        for dy, dx in diagonals:

            @pl.when(exists(dy, dx))
            def _():
                pl.semaphore_signal(
                    barrier, inc=1, device_id=(gy + dy, gx + dx), device_id_type=MESH
                )

        def place(field, value):
            fld[field, centre, :, 0:cols] = value.astype(jnp.float32).reshape(strips, 8, cols)

        lane = lax.broadcasted_iota(jnp.int32, (8, 128), 1)
        sub = lax.broadcasted_iota(jnp.int32, (8, width), 0)
        sub_own = lax.broadcasted_iota(jnp.int32, (8, cols), 0)
        hi = RIM + strips

        for load in loads[:5]:
            load.wait()
        place(MASK, mask_in[...])
        place(BETA, beta_in[...])
        place(SLU, slope_in[0])
        place(SLV, slope_in[1])
        place(H1, thick_in[1])
        place(U1, vel_in[1, 0])
        place(V1, vel_in[1, 1])

        for up in range(2):
            at, row = (RIM + 1, 0) if up else (hi - 2, 6)
            for strip in range(2):
                packed = jnp.zeros((8, cols), jnp.float32)
                for i in range(min(4, DEEP - 4 * strip)):
                    x = fld[4 * strip + i, at, :, 0:cols]
                    move = (2 * i - row) % 8
                    if move:
                        x = pltpu.roll(x, move, 0)
                    inside = jnp.logical_and(sub_own >= 2 * i, sub_own < 2 * i + 2)
                    packed = jnp.where(inside, x, packed)
                row_send[up, strip] = packed

        def begin(plan, base):
            copies = []
            for i, (dy, dx, src, dst) in enumerate(plan):
                copy = pltpu.make_async_remote_copy(
                    src_ref=src, dst_ref=dst,
                    send_sem=send_sem.at[base + i], recv_sem=recv_sem.at[base + i],
                    device_id=(gy + dy, gx + dx), device_id_type=MESH,
                )
                copies.append((dy, dx, copy))

                @pl.when(exists(dy, dx))
                def _():
                    copy.start()

            return copies

        def arrived(copies):
            for dy, dx, copy in copies:

                @pl.when(exists(-dy, -dx))
                def _():
                    copy.wait_recv()

        def row_plan(fields):
            return [
                (-1, 0, fld.at[fields, RIM, :, 0:cols], fld.at[fields, hi, :, 0:cols]),
                (1, 0, fld.at[fields, hi - 1, :, 0:cols], fld.at[fields, RIM - 1, :, 0:cols]),
            ]

        def col_plan(tile):
            send, recv = col_send.at[tile], col_recv.at[tile]
            plan = []
            for side, dx in ((0, -1), (1, 1)):
                plan.append((0, dx, send.at[side], recv.at[side, centre]))
                plan.append((-1, dx, send.at[side, 0:2], recv.at[side, hi : hi + 2]))
                plan.append((1, dx, send.at[side, strips - 2 : strips], recv.at[side, 0:2]))
            return plan

        per_tile = 128 // COLS

        def pack(tile):
            def pack_body(k, _):
                for side, at in ((0, 0), (1, cols - 128)):
                    packed = jnp.zeros((8, 128), jnp.float32)
                    for i in range(per_tile):
                        x = fld[tile * per_tile + i, k + RIM, :, at : at + 128]
                        move = (i * COLS - (0 if side == 0 else 128 - COLS)) % 128
                        if move:
                            x = pltpu.roll(x, move, 1)
                        inside = jnp.logical_and(lane >= i * COLS, lane < (i + 1) * COLS)
                        packed = jnp.where(inside, x, packed)
                    col_send[tile, side, k] = packed
                return 0

            lax.fori_loop(0, strips, pack_body, 0, unroll=4)

        def unpack(tile):
            def unpack_body(k, _):
                nxt, prv = col_recv[tile, 0, k], col_recv[tile, 1, k]
                for i in range(per_tile):
                    a = pltpu.roll(nxt, (-i * COLS) % 128, 1) if i else nxt
                    move = (128 - COLS - i * COLS) % 128
                    b = pltpu.roll(prv, move, 1) if move else prv
                    both = jnp.where(lane < COLS, a, jnp.where(lane >= 128 - COLS, b, 0.0))
                    fld[tile * per_tile + i, k, :, cols:width] = both
                return 0

            lax.fori_loop(0, total, unpack_body, 0, unroll=4)

        def spread(which, axis):
            buf, ssem, rsem, count = (
                (sum_x, sx_send, sx_recv, nx) if axis == "gx" else (sum_y, sy_send, sy_recv, ny)
            )
            made = []
            for off in range(1, count):
                peer = (
                    (gy, lax.rem(gx + off, nx)) if axis == "gx" else (lax.rem(gy + off, ny), gx)
                )
                made.append(
                    pltpu.make_async_remote_copy(
                        src_ref=buf.at[which, 0], dst_ref=buf.at[which, off],
                        send_sem=ssem.at[which, off], recv_sem=rsem.at[which, off],
                        device_id=peer, device_id_type=MESH,
                    )
                )
            return made

        def added(which, axis, n):
            buf, me, count = (sum_x, gx, nx) if axis == "gx" else (sum_y, gy, ny)
            acc = jnp.zeros((8, 128), jnp.float32)
            for src in range(count):
                acc = acc + buf[which, lax.rem(me - src + count, count), n]
            return acc

        def whole(tile):
            return jnp.sum(jnp.sum(tile, axis=1, keepdims=True), axis=0, keepdims=True)

        for load in loads[5:]:
            load.wait()
        place(FLAGS, flags_in[...])
        place(H0, thick_in[0])
        place(U0, vel_in[0, 0])
        place(V0, vel_in[0, 1])
        place(OU0, obs_in[0, 0])
        place(OV0, obs_in[0, 1])
        place(OU1, obs_in[1, 0])
        place(OV1, obs_in[1, 1])
        place(ADJ, adj_in[...])
        pack(0)
        for n, (ou, ov) in enumerate(((OU0, OV0), (OU1, OV1))):
            def scale_body(k, acc, ou=ou, ov=ov):
                a, b = fld[ou, k, :, 0:cols], fld[ov, k, :, 0:cols]
                t = jnp.where(fld[MASK, k, :, 0:cols] == 2.0, a * a + b * b, 0.0)
                for c in range(0, cols, 128):
                    acc = acc + t[:, c : c + 128]
                return acc

            sum_x[0, 0, n] = lax.fori_loop(
                RIM, RIM + strips, scale_body, jnp.zeros((8, 128), jnp.float32), unroll=4
            )

        pack(1)
        beside = [
            jnp.where(at > 0, 1, 0) + jnp.where(at < count - 1, 1, 0)
            for at, count in ((gy, ny), (gx, nx))
        ]
        pl.semaphore_wait(barrier, (nx - 1) + (ny - 1) + beside[0] * beside[1])

        near = begin(
            row_plan(slice(0, DEEP))
            + [(-1, 0, row_send.at[1], row_recv.at[1]), (1, 0, row_send.at[0], row_recv.at[0])],
            0,
        )
        near += begin(col_plan(0), 4)
        scale_x = spread(0, "gx")
        for copy in scale_x:
            copy.start()

        far = begin(row_plan(slice(DEEP, FIELDS)), 10)
        far += begin(col_plan(1), 12)

        arrived(near)
        unpack(0)
        for up in range(2):
            at, row = (hi + 1, 0) if up else (0, 6)
            for strip in range(2):
                packed = row_recv[up, strip]
                for i in range(min(4, DEEP - 4 * strip)):
                    move = (row - 2 * i) % 8
                    x = pltpu.roll(packed, move, 0) if move else packed
                    inside = jnp.logical_and(sub_own >= row, sub_own < row + 2)
                    fld[4 * strip + i, at, :, 0:cols] = jnp.where(inside, x, 0.0)

        for copy in scale_x:
            copy.wait_recv()
        for n in range(2):
            sum_y[0, 0, n] = added(0, "gx", n)
        scale_y = spread(0, "gy")
        for copy in scale_y:
            copy.start()

        def east(x):
            return pltpu.roll(x, width - 1, 1)

        def west(x):
            return pltpu.roll(x, 1, 1)

        def south(cur, nxt):
            return pltpu.roll(jnp.where(sub == 0, nxt, cur), 7, 0)

        def north(prev, cur):
            return pltpu.roll(jnp.where(sub == 7, prev, cur), 1, 0)

        zero = jnp.zeros((8, width), jnp.float32)

        def after(k):
            return jnp.minimum(k + 1, total - 1)

        def static_body(k, _):
            mask = fld[MASK, k]
            cov = jnp.where(mask > 0.0, 1.0, 0.0)
            cov_n = jnp.where(fld[MASK, after(k)] > 0.0, 1.0, 0.0)
            gr = jnp.where(mask == 2.0, 1.0, 0.0)
            cce = 0.5 * cov * east(cov)
            ccs = 0.5 * cov * south(cov, cov_n)
            s["cov"][k] = cov
            s["gr"][k] = gr
            s["fri"][k] = fld[BETA, k] * gr
            s["cce"][k] = cce
            s["ccs"][k] = ccs
            h = fld[H1, k]
            s["1ce"][k] = cce * (h + east(h))
            s["1cs"][k] = ccs * (h + south(h, fld[H1, after(k)]))
            return 0

        lax.fori_loop(0, total, static_body, 0, unroll=4)

        def later_body(k, _):
            flags, h = fld[FLAGS, k], fld[H0, k]
            ds = jnp.where(flags >= 2.0, 1.0, 0.0)
            s["ds"][k] = ds
            s["de"][k] = flags - 2.0 * ds
            s["0ce"][k] = s["cce"][k] * (h + east(h))
            s["0cs"][k] = s["ccs"][k] * (h + south(h, fld[H0, k + 1]))
            return 0

        H = (H0, H1)
        W = ((U0, V0), (U1, V1))

        def velocity(n, j):
            if j == 0:
                return fld.at[W[n][0]], fld.at[W[n][1]]
            return s[f"{n}u{j}"], s[f"{n}v{j}"]

        def edge_zero(names):
            for name in names:
                for k in (first - 1, last):
                    s[name][k] = zero

        edge_zero([f"{n}{c}{j}" for n in range(2) for j in (1, 2, 3) for c in "uv"])
        edge_zero([f"b{b}{c}" for b in range(2) for c in ("qu", "qv", "e")] + ["g1"])

        def forward(n, j, lo, end):
            u_ref, v_ref = velocity(n, j)
            u_to, v_to = velocity(n, j + 1)
            t = {name: s[f"{n}{j}{name}"] for name in SWEEP}

            def body(k, carry):
                pfu, pfv, pc = carry
                kn = after(k)
                u, v = u_ref[k], v_ref[k]
                deu, dev = east(u) - u, east(v) - v
                dsu, dsv = south(u, u_ref[kn]) - u, south(v, v_ref[kn]) - v
                pe = jnp.exp(jnp.log(1.0 + (deu * deu + dev * dev)) * (-1.0 / 3.0))
                ps = jnp.exp(jnp.log(1.0 + (dsu * dsu + dsv * dsv)) * (-1.0 / 3.0))
                ce, cs = s[f"{n}ce"][k] * pe, s[f"{n}cs"][k] * ps
                feu, fev, fsu, fsv = ce * deu, ce * dev, cs * dsu, cs * dsv
                fri, h = s["fri"][k], fld[H[n], k]
                inv = 1.0 / (1.0 + fri + ((ce + west(ce)) + (cs + north(pc, cs))))
                ru = h * fld[SLU, k] - fri * u + ((feu - west(feu)) + (fsu - north(pfu, fsu)))
                rv = h * fld[SLV, k] - fri * v + ((fev - west(fev)) + (fsv - north(pfv, fsv)))
                yu, yv = ru * inv, rv * inv
                cov = s["cov"][k]
                u_to[k] = cov * (u + RELAXATION * yu)
                v_to[k] = cov * (v + RELAXATION * yv)
                for name, value in zip(SWEEP, (pe, ps, deu, dev, dsu, dsv, yu, yv, inv)):
                    t[name][k] = value
                return fsu, fsv, cs

            lax.fori_loop(lo, end, body, (zero, zero, zero), unroll=6 if end - lo == total else 5)

        forward(1, 0, 0, total)
        forward(1, 1, first, last)
        forward(1, 2, first, last)
        arrived(far)
        unpack(1)
        lax.fori_loop(first, last, later_body, 0, unroll=5)
        forward(0, 0, first, last)
        forward(0, 1, first, last)
        forward(0, 2, first, last)

        O = ((OU0, OV0), (OU1, OV1))
        for n in range(2):
            def misfit_body(k, acc, n=n):
                a = s[f"{n}u3"][k, :, 0:cols] - fld[O[n][0], k, :, 0:cols]
                b = s[f"{n}v3"][k, :, 0:cols] - fld[O[n][1], k, :, 0:cols]
                t = s["gr"][k, :, 0:cols] * (a * a + b * b)
                for c in range(0, cols, 128):
                    acc = acc + t[:, c : c + 128]
                return acc

            sum_x[1, 0, n] = 0.5 * lax.fori_loop(
                RIM, RIM + strips, misfit_body, jnp.zeros((8, 128), jnp.float32), unroll=4
            )
        misfit_x = spread(1, "gx")
        for copy in misfit_x:
            copy.start()

        for copy in scale_y:
            copy.wait_recv()
        scales = [whole(added(0, "gy", n)) * (1.0 / cell_count) + EPSILON for n in range(2)]

        def emit(n, j, b, k, lu, lv):
            cov, fri = s["cov"][k], s["fri"][k]
            au, av = cov * lu, cov * lv
            inv = RELAXATION * s[f"{n}{j}inv"][k]
            qu, qv = au * inv, av * inv
            s[f"b{b}qu"][k] = qu
            s[f"b{b}qv"][k] = qv
            s[f"b{b}e"][k] = -(qu * s[f"{n}{j}yu"][k] + qv * s[f"{n}{j}yv"][k])
            s[f"b{b}bu"][k] = au - fri * qu
            s[f"b{b}bv"][k] = av - fri * qv

        def transport(n, g_ref):
            per_scale = jnp.broadcast_to(1.0 / scales[n], (8, width))

            def body(k, carry):
                pvs, phs = carry
                kn = k + 1
                g, gn = s["cov"][k] * g_ref[k], s["cov"][kn] * g_ref[kn]
                h, hn = fld[H[n], k], fld[H[n], kn]
                u, v = s[f"{n}u3"][k], s[f"{n}v3"][k]
                de, ds = s["de"][k], s["ds"][k]
                pse = (TIME_STEP * s["cce"][k]) * (east(g) - g)
                pss = (TIME_STEP * s["ccs"][k]) * (south(g, gn) - g)
                ue = pse * (de * h + (1.0 - de) * east(h))
                vs = pss * (ds * h + (1.0 - ds) * south(h, hn))
                he = pse * (u + east(u))
                hs = pss * (v + south(v, s[f"{n}v3"][kn]))
                he_here, hs_here = de * he, ds * hs
                he_there, hs_there = he - he_here, hs - hs_here
                seed = s["gr"][k] * per_scale
                lu = seed * (u - fld[O[n][0], k]) + (ue + west(ue))
                lv = seed * (v - fld[O[n][1], k]) + (vs + north(pvs, vs))
                s["hacc"][k] = g + (he_here + west(he_there)) + (hs_here + north(phs, hs_there))
                emit(n, 2, 0, k, lu, lv)
                return vs, hs_there

            lax.fori_loop(first, last, body, (zero, zero), unroll=5)

        def backward(n, j, b, end, g_to=None, f_to=None):
            u_ref, v_ref = velocity(n, j)
            t = {name: s[f"{n}{j}{name}"] for name in SWEEP}
            q = {name: s[f"b{b}{name}"] for name in BACK}
            start, finish = j == 2, j == 0

            def body(k, carry):
                kn = k + 1
                qu, qv, e = q["qu"][k], q["qv"][k], q["e"][k]
                feu, fev = qu - east(qu), qv - east(qv)
                fsu, fsv = qu - south(qu, q["qu"][kn]), qv - south(qv, q["qv"][kn])
                pe, ps = t["pe"][k], t["ps"][k]
                deu, dev, dsu, dsv = t["deu"][k], t["dev"][k], t["dsu"][k], t["dsv"][k]
                ke = (feu * deu + fev * dev) + (e + east(e))
                ks = (fsu * dsu + fsv * dsv) + (e + south(e, q["e"][kn]))
                kpe, kps = ke * pe, ks * ps
                f = e - (qu * u_ref[k] + qv * v_ref[k])
                h = qu * fld[SLU, k] + qv * fld[SLV, k] + s["hacc"][k]
                if not start:
                    kpe_sum, kps_sum = s["hce"][k] + kpe, s["hcs"][k] + kps
                    f = f + s["facc"][k]
                else:
                    kpe_sum, kps_sum = kpe, kps
                if finish:
                    ge, gs = s["cce"][k] * kpe_sum, s["ccs"][k] * kps_sum
                    g_to[k] = h + ((ge + west(ge)) + (gs + north(carry[0], gs)))
                    f_to[k] = f
                    return (gs,)
                s["hce"][k] = kpe_sum
                s["hcs"][k] = kps_sum
                s["facc"][k] = f
                s["hacc"][k] = h
                ce, cs = s[f"{n}ce"][k] * pe, s[f"{n}cs"][k] * ps
                te = (2.0 / 3.0) * ce * (pe * pe) * kpe
                ts = (2.0 / 3.0) * cs * (ps * ps) * kps
                xeu, xev = ce * feu - te * deu, ce * fev - te * dev
                xsu, xsv = cs * fsu - ts * dsu, cs * fsv - ts * dsv
                lu = q["bu"][k] + ((west(xeu) - xeu) + (north(carry[0], xsu) - xsu))
                lv = q["bv"][k] + ((west(xev) - xev) + (north(carry[1], xsv) - xsv))
                emit(n, j - 1, 1 - b, k, lu, lv)
                return xsu, xsv

            lax.fori_loop(first, end, body, (zero,) if finish else (zero, zero), unroll=5)

        transport(1, fld.at[ADJ])
        backward(1, 2, 0, last)
        backward(1, 1, 1, last)
        backward(1, 0, 0, last, s["g1"], s["f1"])

        for copy in misfit_x:
            copy.wait_recv()
        for n in range(2):
            sum_y[1, 0, n] = added(1, "gx", n)
        misfit_y = spread(1, "gy")
        for copy in misfit_y:
            copy.start()

        transport(0, s["g1"])
        backward(0, 2, 0, last)
        backward(0, 1, 1, last)
        backward(0, 0, 0, last, s["g0"], s["f0"])

        f_sum = s["f1"][centre, :, 0:cols] + s["f0"][centre, :, 0:cols]
        beta_out[...] = s["gr"][centre, :, 0:cols] * f_sum
        thick_out[...] = s["g0"][centre, :, 0:cols]

        for copy in misfit_y:
            copy.wait_recv()
        parts = [whole(added(1, "gy", n)) * (1.0 / cell_count) / scales[n] for n in range(2)]
        misfit_out[...] = parts[1] + parts[0]
        for dy, dx, copy in near + far:

            @pl.when(exists(dy, dx))
            def _():
                copy.wait_send()
        for copy in scale_x + scale_y + misfit_x + misfit_y:
            copy.wait_send()

    return kernel


def on_device(*args):
    ny, nx = lax.axis_size("gy"), lax.axis_size("gx")
    rows, cols = args[3].shape
    strips = rows // 8
    total = strips + 2 * RIM
    width = cols + 128
    vmem = pl.BlockSpec(memory_space=pltpu.VMEM)
    dma = pltpu.SemaphoreType.DMA
    beta, thick, misfit = pl.pallas_call(
        make_kernel(ny, nx, rows, cols, rows * cols * ny * nx),
        out_shape=(
            pltpu.VMEM((strips, 8, cols), jnp.float32),
            pltpu.VMEM((strips, 8, cols), jnp.float32),
            jax.ShapeDtypeStruct((1, 1), jnp.float32),
        ),
        in_specs=[pl.BlockSpec(memory_space=pltpu.HBM)] * len(args),
        out_specs=(vmem, vmem, vmem),
        scratch_shapes=[
            pltpu.VMEM((FIELDS, total, 8, width), jnp.float32),
            pltpu.VMEM((FIELDS * COLS // 128, 2, strips, 8, 128), jnp.float32),
            pltpu.VMEM((FIELDS * COLS // 128, 2, total, 8, 128), jnp.float32),
            pltpu.VMEM((2, 2, 8, cols), jnp.float32),
            pltpu.VMEM((2, 2, 8, cols), jnp.float32),
            pltpu.VMEM((2, nx, 2, 8, 128), jnp.float32),
            pltpu.VMEM((2, ny, 2, 8, 128), jnp.float32),
            dma((18,)), dma((18,)),
            dma((2, nx)), dma((2, nx)), dma((2, ny)), dma((2, ny)), dma((len(args),)),
        ]
        + [pltpu.VMEM(arg.shape, arg.dtype) for arg in args]
        + [pltpu.VMEM((total, 8, width), jnp.float32)] * len(NAMES),
        compiler_params=pltpu.CompilerParams(
            collective_id=0, has_side_effects=True, vmem_limit_bytes=62 * 1024 * 1024
        ),
    )(*args)
    return beta.reshape(rows, cols), thick.reshape(rows, cols), misfit.reshape(())


def solution(mesh):
    in_specs = (
        P(None, "gy", "gx"),
        P(None, None, "gy", "gx"),
        P(None, "gy", "gx"),
        P("gy", "gx"),
        P("gy", "gx"),
        P("gy", "gx"),
        P(None, None, "gy", "gx"),
        P("gy", "gx"),
    )
    out_specs = (P("gy", "gx"), P("gy", "gx"), P())
    return jax.shard_map(
        on_device, mesh=mesh, in_specs=in_specs, out_specs=out_specs, check_vma=False
    )
```
